32 devices in a mesh: row: 4 (over z), col: 4 (over y, x), rep: 2 (over core).
Axes of the slice: x: 2, y: 2, z: 4, core: 2. Of those that a mesh axis runs over, the one named last changes fastest.
Arguments:
- tokens: bfloat16 [3072, 5120], P('row'), may hold values from -6 to 6
- up_weight: bfloat16 [5120, 10240], P('row', 'col'), may hold values from -0.125 to 0.125
- block_mask: int32 [80, 160], replicated, may hold values from 0 to 1
Outputs:
- hidden: bfloat16 [3072, 10240], P('row', ('col', 'rep'))
The draws below stay inside these ranges and needn't reach their ends.
All inputs are finite; a program needn't handle non-finite values.
Results may differ from the reference program's by a relative error of at most 0.001.
Values may be sent and summed in bfloat16 or wider, within the bound.
No kernel may reach another device: no remote copies, remote signals or barrier semaphores. Data moves between devices by JAX's collectives and lax.ppermute only.
A program may use at most 64 MiB of HBM per device.

```python
import jax
import jax.numpy as jnp

D = 5120
FF = 10240
BLOCK = 64
TOKENS = 3072
GROUP_BLOCKS = 40


def draw_block_mask(key, part):
    block_rows = D // BLOCK
    block_cols = FF // BLOCK
    key_level, key_roll, key_dense = jax.random.split(jax.random.fold_in(key, 71), 3)
    levels = jax.random.randint(key_level, (block_cols,), 0, 8)
    rolls = jax.random.randint(key_roll, (block_rows, block_cols), 0, 8)
    dense_group = jax.random.randint(key_dense, (), 0, block_cols // GROUP_BLOCKS)
    group_ids = jnp.arange(block_cols, dtype=jnp.int32) // GROUP_BLOCKS
    keep = (rolls < levels[None, :]) | (group_ids == dense_group)[None, :]
    return keep.astype(jnp.int32)


def shard_levels(rng, extent, shards, low, top_value):
    gain, own = 1.0, jax.random.fold_in(rng, 6)
    for dim, shards_of in shards:
        steps = jnp.exp(jax.random.uniform(jax.random.fold_in(own, dim), (shards_of,), jnp.float32, low / len(shards), top_value / len(shards)))
        gain = gain * jnp.repeat(steps, extent[dim] // shards_of).reshape([-1 if axis == dim else 1 for axis in range(len(extent))])
    return gain


def gaussian(key, shape, scale, reach, cuts=(), kind=jnp.bfloat16):
    drawn = scale * jax.random.normal(key, shape, jnp.float32)
    if cuts:
        drawn = drawn * shard_levels(key, shape, cuts, -0.22, 0.18)
    return jnp.clip(drawn, -reach, reach).astype(kind)


def setup_inputs(seed: int = 0) -> dict:
    keys = jax.random.split(jax.random.key(seed), 4)
    tokens = gaussian(keys[0], (TOKENS, D), 1.0, 6.0, ((0, 4),))
    up_weight = gaussian(keys[1], (D, FF), (D // 2) ** -0.5, 0.125, ((0, 4), (1, 4)))
    block_mask = draw_block_mask(jax.random.fold_in(keys[3], 71), 0)
    return {"tokens": tokens, "up_weight": up_weight, "block_mask": block_mask}


def reference(tokens, up_weight, block_mask):
    keep = jnp.repeat(jnp.repeat(block_mask.astype(jnp.bfloat16), BLOCK, axis=0), BLOCK, axis=1)
    masked_weight = up_weight * keep
    preact = jnp.dot(tokens, masked_weight, preferred_element_type=jnp.float32)
    return jax.nn.gelu(preact, approximate=True).astype(jnp.bfloat16)
```

```python
import functools

import jax
import jax.numpy as jnp
from jax import lax
from jax.experimental import pallas as pl
from jax.experimental.pallas import tpu as pltpu
from jax.sharding import PartitionSpec as P

BLOCK = 64
CHUNK = 256


def gather_body(tokens, up_weight, block_mask):
    weight_rows_dev, hidden_dev = up_weight.shape
    rep_count = lax.axis_size("rep")
    row_index = lax.axis_index("row")
    col_index = lax.axis_index("col")
    rep_index = lax.axis_index("rep")
    row_ids = row_index * weight_rows_dev + lax.iota(jnp.int32, weight_rows_dev)
    col_ids = col_index * hidden_dev + lax.iota(jnp.int32, hidden_dev)
    row_onehot = (
        row_ids[:, None] // BLOCK == lax.iota(jnp.int32, block_mask.shape[0])[None, :]
    ).astype(jnp.float32)
    col_onehot = (
        col_ids[:, None] // BLOCK == lax.iota(jnp.int32, block_mask.shape[1])[None, :]
    ).astype(jnp.float32)
    mask_rows = jnp.dot(row_onehot, block_mask.astype(jnp.float32), precision=lax.Precision.HIGHEST)
    local_mask = jnp.dot(mask_rows, col_onehot.T, precision=lax.Precision.HIGHEST)
    masked_weight = up_weight * local_mask.astype(jnp.bfloat16)
    share = hidden_dev // rep_count
    my_columns = lax.dynamic_slice_in_dim(masked_weight, rep_index * share, share, 1)
    preact = jnp.dot(
        tokens,
        lax.all_gather(my_columns, "row", axis=0, tiled=True),
        preferred_element_type=jnp.float32,
    )
    return jax.nn.gelu(preact, approximate=True).astype(jnp.bfloat16)


def mask_kernel(place, mask, w_ref, *out_refs):
    row_blocks, tiles = w_ref.shape[0] // BLOCK, w_ref.shape[1] // (2 * BLOCK)
    lane = lax.broadcasted_iota(jnp.int32, (BLOCK, 2 * BLOCK), 1)
    per = CHUNK // (2 * BLOCK)

    for chunk, out in enumerate(out_refs):
        def step(i, _):
            for t in range(per):
                tile = chunk * per + t
                col = place[1] + 2 * tile
                left = mask[place[0] + i, col]
                right = mask[place[0] + i, col + 1]
                rows = pl.ds(pl.multiple_of(i * BLOCK, BLOCK), BLOCK)
                keep = jnp.where(lane < BLOCK, left, right)
                value = w_ref[rows, tile * 2 * BLOCK : (tile + 1) * 2 * BLOCK]
                out[rows, t * 2 * BLOCK : (t + 1) * 2 * BLOCK] = value * keep.astype(jnp.bfloat16)
            return 0

        lax.fori_loop(0, row_blocks, step, 0)


def masked_chunks(place, mask, weight, share, rep_index):
    rows = weight.shape[0]
    chunks = share // CHUNK
    return pl.pallas_call(
        mask_kernel,
        grid_spec=pltpu.PrefetchScalarGridSpec(
            num_scalar_prefetch=2,
            grid=(1,),
            in_specs=[pl.BlockSpec((rows, share), lambda i, place, mask: (0, place[2]))],
            out_specs=[pl.BlockSpec((rows, CHUNK), lambda i, place, mask: (0, 0))] * chunks,
        ),
        out_shape=[jax.ShapeDtypeStruct((rows, CHUNK), jnp.bfloat16)] * chunks,
        compiler_params=pltpu.CompilerParams(vmem_limit_bytes=40 * 2**20),
    )(place, mask, weight)


INWARD = [(0, 1), (3, 2)]
OUTWARD = [(1, 0), (2, 3)]
MIDDLE = [(1, 2), (2, 1)]
SWAP_X = [(0, 1), (1, 0), (2, 3), (3, 2)]
SWAP_Y = [(0, 2), (2, 0), (1, 3), (3, 1)]
SWAP_CORE = [(0, 1), (1, 0)]


def line_body(tokens, up_weight, block_mask):
    depth, hidden_dev = up_weight.shape
    row_count, rep_count = lax.axis_size("row"), lax.axis_size("rep")
    col_count = lax.axis_size("col")
    r, c, p = (lax.axis_index(a).astype(jnp.int32) for a in ("row", "col", "rep"))
    share = hidden_dev // rep_count
    chunks = share // CHUNK
    width = tokens.shape[1]

    parts = col_count * rep_count
    piece = width // parts
    mine = lax.dynamic_slice_in_dim(tokens, (c * rep_count + p) * piece, piece, 1)
    mine = lax.ppermute(mine, "row", INWARD)
    half = tokens.shape[0] // 2
    a, b = mine[:half], mine[half:]
    ax = lax.ppermute(a, "col", SWAP_X)
    by = lax.ppermute(b, "col", SWAP_Y)
    a2, b2 = jnp.stack([a, ax]), jnp.stack([b, by])
    ay = lax.ppermute(a2, "col", SWAP_Y)
    bx = lax.ppermute(b2, "col", SWAP_X)
    four = jnp.concatenate(
        [
            jnp.concatenate([a2, ay], 0),
            jnp.stack([b, bx[0], by, bx[1]]),
        ],
        1,
    )
    four_other = lax.ppermute(four, "rep", SWAP_CORE)
    both = jnp.stack([four, four_other], 1)
    order = [
        lax.dynamic_index_in_dim(
            both.reshape(parts, tokens.shape[0], piece), ((i // rep_count) ^ c) * rep_count + ((i % rep_count) ^ p), 0, False
        )
        for i in range(parts)
    ]
    tokens_end = jnp.concatenate(order, 1)

    place = jnp.stack([r * (depth // BLOCK), (c * rep_count + p) * (share // BLOCK), p])
    own = masked_chunks(place, block_mask, up_weight, share, p)
    middle = lax.ppermute(jnp.stack(own), "row", MIDDLE)
    near = [lax.ppermute(w, "row", INWARD) for w in own]
    far = [lax.ppermute(w, "row", MIDDLE) for w in near]

    is_one = r <= 1
    def ordered(i):
        first = jnp.concatenate([near[i], own[i], middle[i], far[i]], 0)
        second = jnp.concatenate([far[i], middle[i], own[i], near[i]], 0)
        return jnp.where(is_one, first, second)

    def hidden(t, w):
        preact = jnp.dot(t, w, preferred_element_type=jnp.float32)
        return jax.nn.gelu(preact, approximate=True).astype(jnp.bfloat16)

    is_middle = (r == 1) | (r == 2)
    out = []
    for i in range(chunks):
        w = ordered(i)
        here = hidden(tokens, w)
        back = lax.ppermute(hidden(tokens_end, w), "row", OUTWARD)
        out.append(jnp.where(is_middle, here, back))
    return jnp.concatenate(out, 1)


def solution(mesh):
    in_specs = (P("row", None), P("row", "col"), P())
    out_specs = P("row", ("col", "rep"))
    line = dict(mesh.shape) == {"row": 4, "col": 4, "rep": 2}
    body = line_body if line else gather_body
    return jax.shard_map(body, mesh=mesh, in_specs=in_specs, out_specs=out_specs, check_vma=False)
```

```python
import functools

import jax
import jax.numpy as jnp
from jax import lax
from jax.experimental import pallas as pl
from jax.experimental.pallas import tpu as pltpu
from jax.sharding import PartitionSpec as P

BLOCK = 64


def gather_body(tokens, up_weight, block_mask):
    weight_rows_dev, hidden_dev = up_weight.shape
    rep_count = lax.axis_size("rep")
    row_index = lax.axis_index("row")
    col_index = lax.axis_index("col")
    rep_index = lax.axis_index("rep")
    row_ids = row_index * weight_rows_dev + lax.iota(jnp.int32, weight_rows_dev)
    col_ids = col_index * hidden_dev + lax.iota(jnp.int32, hidden_dev)
    row_onehot = (
        row_ids[:, None] // BLOCK == lax.iota(jnp.int32, block_mask.shape[0])[None, :]
    ).astype(jnp.float32)
    col_onehot = (
        col_ids[:, None] // BLOCK == lax.iota(jnp.int32, block_mask.shape[1])[None, :]
    ).astype(jnp.float32)
    mask_rows = jnp.dot(row_onehot, block_mask.astype(jnp.float32), precision=lax.Precision.HIGHEST)
    local_mask = jnp.dot(mask_rows, col_onehot.T, precision=lax.Precision.HIGHEST)
    masked_weight = up_weight * local_mask.astype(jnp.bfloat16)
    share = hidden_dev // rep_count
    my_columns = lax.dynamic_slice_in_dim(masked_weight, rep_index * share, share, 1)
    preact = jnp.dot(
        tokens,
        lax.all_gather(my_columns, "row", axis=0, tiled=True),
        preferred_element_type=jnp.float32,
    )
    return jax.nn.gelu(preact, approximate=True).astype(jnp.bfloat16)


UP = [(0, 1), (1, 2), (2, 3)]
DOWN = [(3, 2), (2, 1), (1, 0)]
INWARD = [(0, 1), (3, 2)]
OUTWARD = [(1, 0), (2, 3)]
MIDDLE = [(1, 2), (2, 1)]
SWAP_X = [(0, 1), (1, 0), (2, 3), (3, 2)]
SWAP_Y = [(0, 2), (2, 0), (1, 3), (3, 1)]
SWAP_DIAGONAL = [(0, 3), (3, 0), (1, 2), (2, 1)]
SWAPS = (SWAP_X, SWAP_Y, SWAP_DIAGONAL)
SWAP_CORE = [(0, 1), (1, 0)]
CHIPS = 4
CORES = 2
OWN = 20
SPARE = 4
SLOTS = OWN + SPARE
LIGHT = 16
HEAVY = (SLOTS - LIGHT) // 2
CAP = 66
TILE = 2 * BLOCK
EMPTY = CHIPS * CORES * OWN
ROW_TILE = 384
SIZE = CAP * BLOCK
MIB = 2**20
BRIEF = pl.CostEstimate(flops=1, bytes_accessed=1, transcendentals=0)


def after(value, *earlier):
    return lax.optimization_barrier((value, *earlier))[0]


def vmem(limit):
    return pltpu.CompilerParams(vmem_limit_bytes=limit * MIB)


def swap_halves(value):
    return pltpu.roll(value.astype(jnp.float32), BLOCK, 1).astype(jnp.bfloat16)


def make_plan(count, key, table, shared, c, p):
    loads = []
    for group in range(CHIPS * CORES):
        total = count[group * OWN]
        for i in range(1, OWN):
            total += count[group * OWN + i]
        loads.append(total)
    chip = [loads[2 * i] + loads[2 * i + 1] for i in range(CHIPS)]
    h, best = jnp.int32(0), chip[0]
    for i in range(1, CHIPS):
        more = chip[i] > best
        h, best = jnp.where(more, i, h), jnp.where(more, chip[i], best)
    shared[0] = h
    taken = []
    for core in range(CORES):
        mine = [loads[2 * i + core] for i in range(CHIPS)]
        heavy = sum(jnp.where(h == i, mine[i], 0) for i in range(CHIPS))

        def given(kept):
            out = []
            for i in range(CHIPS):
                spare = heavy * kept - OWN * mine[i]
                n = sum((spare >= k * heavy).astype(jnp.int32) for k in range(1, SPARE + 1))
                out.append(jnp.where(h == i, 0, n))
            return out

        kept = lax.while_loop(
            lambda kept: OWN - sum(given(kept)) > kept, lambda kept: kept + 1, jnp.int32(OWN - 3 * SPARE)
        )
        taken.append(given(kept))
        for i in range(CHIPS):
            shared[1 + CORES * i + core] = taken[core][i]
    taken = [jnp.where(p == 0, first, second) for first, second in zip(*taken)]
    order = [jnp.where(h <= k, taken[k + 1], taken[k]) for k in range(CHIPS - 1)]
    extra = sum(jnp.where(c == i, taken[i], 0) for i in range(CHIPS))
    base = (c * CORES + p) * OWN

    gone = []
    for i in range(OWN):
        k, j = i // SPARE, i % SPARE
        gone.append((c == h) & (j < order[k]) if k < CHIPS - 1 else jnp.bool_(False))
        key[i] = jnp.where(gone[i], -1, count[base + i])
    for q in range(SPARE):
        table[q] = EMPTY
        table[SLOTS + q] = 0
    for i in range(OWN):
        rank = jnp.int32(0)
        for j in range(OWN):
            if j != i:
                first = key[j] <= key[i] if j < i else key[j] < key[i]
                rank += first.astype(jnp.int32)
        slot = SPARE - extra + rank
        table[slot] = jnp.where(gone[i], EMPTY, base + i)
        table[SLOTS + slot] = i
        k = min(i // SPARE, CHIPS - 2)
        other = k + (h <= k).astype(jnp.int32)
        back = SLOTS + ((c ^ other) - 1) * SPARE + (SPARE - 1 - i % SPARE)
        table[2 * SLOTS + i] = jnp.where(gone[i], back, slot)
    k = c - (c > h).astype(jnp.int32)
    for i in range(SPARE):

        @pl.when(i < extra)
        def _():
            table[SLOTS - 1 - i] = (h * CORES + p) * OWN + SPARE * k + i
            table[2 * SLOTS - 1 - i] = OWN + i

    table[2 * SLOTS + OWN] = c ^ h


TABLE = 2 * SLOTS + OWN + 1


def pack_kernel(place, mask, count, w_ref, table, shared, packed, own_heavy, key, both, line):
    r, c, p = place[0], place[1], place[2]
    make_plan(count, key, table, shared, c, p)
    row_blocks = w_ref.shape[0] // BLOCK
    for t in range(w_ref.shape[1] // TILE):
        value = w_ref[:, t * TILE : (t + 1) * TILE]
        both[0, :, t * TILE : (t + 1) * TILE] = value
        both[1, :, t * TILE : (t + 1) * TILE] = swap_halves(value)
    side = lax.broadcasted_iota(jnp.int32, (BLOCK, TILE), 1) // BLOCK

    def lanes(source):
        return pl.ds(pl.multiple_of((source >> 1) * TILE, TILE), TILE)

    def column(q, s):
        col = table[q]
        source = table[SLOTS + q]
        for i in range(row_blocks):
            at = jnp.minimum(s, 2 * CAP)
            value = both[(source ^ at) & 1, i * BLOCK : (i + 1) * BLOCK, lanes(source)]
            line[pl.ds(pl.multiple_of(at * BLOCK, BLOCK), BLOCK), :] = value
            s = s + mask[r * row_blocks + i, col]
        return s

    lax.fori_loop(0, LIGHT, column, jnp.int32(0))
    for n in range(CAP):
        left = line[2 * n * BLOCK : (2 * n + 1) * BLOCK, :]
        right = line[(2 * n + 1) * BLOCK : (2 * n + 2) * BLOCK, :]
        packed[n * BLOCK : (n + 1) * BLOCK, :] = jnp.where(side == 0, left, right)

    for t in range(HEAVY // 2):
        slots = (LIGHT + 2 * t, LIGHT + 2 * t + 1)

        def block(i, _):
            rows = pl.ds(pl.multiple_of(i * BLOCK, BLOCK), BLOCK)
            values = []
            for half in range(2):
                source, col = table[SLOTS + slots[half]], table[slots[half]]
                value = both[(source & 1) ^ half, rows, lanes(source)]
                values.append(jnp.where(mask[r * row_blocks + i, col] != 0, value, jnp.zeros_like(value)))
            own_heavy[rows, t * TILE : (t + 1) * TILE] = jnp.where(side == 0, values[0], values[1])
            return 0

        lax.fori_loop(0, row_blocks, block, 0)


def pack_columns(place, mask, count, weight):
    depth, share = weight.shape[0], OWN * BLOCK
    smem = pl.BlockSpec(memory_space=pltpu.SMEM)
    return pl.pallas_call(
        pack_kernel,
        grid_spec=pltpu.PrefetchScalarGridSpec(
            num_scalar_prefetch=3,
            grid=(1,),
            in_specs=[pl.BlockSpec((depth, share), lambda i, place, mask, count: (0, place[2]))],
            out_specs=[
                smem,
                smem,
                pl.BlockSpec((CAP * BLOCK, TILE), lambda i, place, mask, count: (0, 0)),
                pl.BlockSpec((depth, HEAVY * BLOCK), lambda i, place, mask, count: (0, 0)),
            ],
            scratch_shapes=[
                pltpu.SMEM((OWN,), jnp.int32),
                pltpu.VMEM((2, depth, share), jnp.bfloat16),
                pltpu.VMEM((2 * SIZE + BLOCK, TILE), jnp.bfloat16),
            ],
        ),
        out_shape=[
            jax.ShapeDtypeStruct((TABLE,), jnp.int32),
            jax.ShapeDtypeStruct((1 + CHIPS * CORES,), jnp.int32),
            jax.ShapeDtypeStruct((CAP * BLOCK, TILE), jnp.bfloat16),
            jax.ShapeDtypeStruct((depth, HEAVY * BLOCK), jnp.bfloat16),
        ],
        cost_estimate=BRIEF,
        compiler_params=vmem(48),
    )(place, mask, count, weight)


def most_packed(counts, count, shared):
    groups = CHIPS * CORES
    column = lax.iota(jnp.int32, groups * OWN)
    group, i = column // OWN, column % OWN
    h, taken = shared[0], shared[1 : 1 + groups]
    to = i // SPARE + (h <= i // SPARE).astype(jnp.int32)
    ways = jnp.sum(jnp.where((to * CORES + group % CORES)[:, None] == lax.iota(jnp.int32, groups), taken, 0), 1)
    gone = (group // CORES == h) & (i < 3 * SPARE) & (i % SPARE < ways)
    key = jnp.where(gone, -1, count)
    before = (key[None, :] < key[:, None]) | ((key[None, :] == key[:, None]) & (column[None, :] < column[:, None]))
    rank = jnp.sum((before & (group[None, :] == group[:, None])).astype(jnp.int32), 1)
    extra = jnp.sum(jnp.where(group[:, None] == lax.iota(jnp.int32, groups), taken, 0), 1)
    light = (SPARE - extra + rank < LIGHT) & ~gone
    return jnp.max(jnp.sum(jnp.where(light, counts, 0).reshape(counts.shape[0], groups, OWN), 2))


def whole_kernel(first, place, mask, table, w_ref, x_ref, y_ref, d_ref, *rest):
    *outs, taken = rest
    r = place[0]
    row_blocks = w_ref.shape[0] // BLOCK
    side = lax.broadcasted_iota(jnp.int32, (BLOCK, TILE), 1) // BLOCK
    for i, ref in enumerate((x_ref, y_ref, d_ref)):

        @pl.when(table[2 * SLOTS + OWN] == i + 1)
        def _():
            taken[...] = ref[...]

    slot = first
    for out in outs:
        for t in range(out.shape[1] // TILE):
            halves = []
            for half in range(2):
                source, col = table[SLOTS + slot], table[slot]
                slot += 1
                own = jnp.minimum(source, OWN - 1)
                other = jnp.maximum(source - OWN, 0)
                halves.append((
                    source >= OWN, col, (source & 1) != half,
                    pl.ds(pl.multiple_of((own >> 1) * TILE, TILE), TILE),
                    pl.ds(pl.multiple_of((other >> 1) * TILE, TILE), TILE),
                ))

            def block(i, _):
                rows = pl.ds(pl.multiple_of(i * BLOCK, BLOCK), BLOCK)
                values = []
                for is_taken, col, swap, own, other in halves:
                    value = jnp.where(is_taken, taken[rows, other], w_ref[rows, own])
                    value = jnp.where(swap, swap_halves(value), value)
                    values.append(jnp.where(mask[r * row_blocks + i, col] != 0, value, jnp.zeros_like(value)))
                out[rows, t * TILE : (t + 1) * TILE] = jnp.where(side == 0, values[0], values[1])
                return 0

            lax.fori_loop(0, row_blocks, block, 0)


def whole_columns(first, widths, place, mask, table, weight, taken):
    rows, width = weight.shape[0], OWN * BLOCK
    full = lambda shape: pl.BlockSpec(shape, lambda i, place, mask, table: (0, 0))
    return pl.pallas_call(
        functools.partial(whole_kernel, first),
        grid_spec=pltpu.PrefetchScalarGridSpec(
            num_scalar_prefetch=3,
            grid=(1,),
            in_specs=[pl.BlockSpec((rows, width), lambda i, place, mask, table: (0, place[2]))]
            + [full(taken[0].shape)] * 3,
            out_specs=[full((rows, w * BLOCK)) for w in widths],
            scratch_shapes=[pltpu.VMEM(taken[0].shape, jnp.bfloat16)],
        ),
        out_shape=[jax.ShapeDtypeStruct((rows, w * BLOCK), jnp.bfloat16) for w in widths],
        cost_estimate=BRIEF,
        compiler_params=vmem(48),
    )(place, mask, table, weight, *taken)


def gelu(preact):
    return jax.nn.gelu(preact, approximate=True).astype(jnp.bfloat16)


def light_sources(me, nearest):
    if nearest:
        return [(me, me >= 0), (me - 1, me >= 1), (me + 1, me <= 2)]
    side = jnp.where(me <= 1, 1, -1)
    return [(me + 2 * side, me >= 0), (me + 3 * side, (me == 0) | (me == 3))]


def light_kernel(nearest, place, mask, table, *rest):
    n = 3 if nearest else 2
    pieces, rest = rest[: n if nearest else 2 * n], rest[n if nearest else 2 * n :]
    if nearest:
        here_ref, total, weight, blocks, lines, sems = rest
    else:
        here_ref, before, out_ref, total, weight, blocks, lines, sems, before_sem = rest
        load = pltpu.make_async_copy(before, total, before_sem)
    step = pl.program_id(0)
    row_blocks = weight.shape[0] // BLOCK
    zero = lines.shape[1] - BLOCK
    me = place[0]
    sources = light_sources(me, nearest)

    def copies(i):
        slot = blocks.at[pl.ds(i * SIZE, SIZE)]
        if nearest:
            return [(sources[i][1], pltpu.make_async_copy(pieces[i], slot, sems.at[i]))]
        return [
            (sources[i][1] & (me <= 1 if k else me > 1), pltpu.make_async_copy(pieces[2 * i + k], slot, sems.at[i]))
            for k in range(2)
        ]

    @pl.when(step == 0)
    def _():
        for i in range(n):
            for there, copy in copies(i):
                pl.when(there)(copy.start)
        for half in range(2):
            lines[half, zero : zero + BLOCK, :] = jnp.zeros((BLOCK, TILE), jnp.bfloat16)
        if nearest:
            total[...] = jnp.zeros_like(total)
        else:
            load.start()

    for i in range(n):
        for there, copy in copies(i):
            pl.when((step == i) & there)(copy.wait)

    source, valid = sources[0]
    for i in range(1, n):
        source = jnp.where(step == i, sources[i][0], source)
        valid = jnp.where(step == i, sources[i][1], valid)

    @pl.when(valid)
    def _():
        side = lax.broadcasted_iota(jnp.int32, (BLOCK, TILE), 1) // BLOCK
        many = 11

        def spread(t, _):
            value = blocks[pl.ds(pl.multiple_of(step * SIZE + t * many * BLOCK, BLOCK), many * BLOCK), :]
            other = swap_halves(value)
            for k in range(many):
                first = pl.ds(pl.multiple_of(2 * (t * many + k) * BLOCK, BLOCK), BLOCK)
                second = pl.ds(pl.multiple_of(2 * (t * many + k) * BLOCK + BLOCK, BLOCK), BLOCK)
                rows = slice(k * BLOCK, (k + 1) * BLOCK)
                lines[0, first, :] = value[rows]
                lines[1, first, :] = other[rows]
                lines[0, second, :] = other[rows]
                lines[1, second, :] = value[rows]
            return 0

        lax.fori_loop(0, CAP // many, spread, 0)

        def pair(t, row):
            cols = [table[2 * t], table[2 * t + 1]]
            kept = [[mask[source * row_blocks + i, col] * BLOCK for i in range(row_blocks)] for col in cols]
            at = [row, row + sum(kept[0])]
            lanes = pl.ds(pl.multiple_of(t * TILE, TILE), TILE)
            for i in range(row_blocks):
                values = []
                for half in range(2):
                    rows = pl.multiple_of(jnp.where(kept[half][i] != 0, at[half], zero), BLOCK)
                    values.append(lines[half, pl.ds(rows, BLOCK), :])
                    at[half] = at[half] + kept[half][i]
                weight[i * BLOCK : (i + 1) * BLOCK, lanes] = jnp.where(side == 0, values[0], values[1])
            return at[1]

        lax.fori_loop(0, LIGHT // 2, pair, jnp.int32(0))
        if not nearest:
            pl.when(step == 0)(load.wait)
        for first in range(0, total.shape[0], ROW_TILE):
            rows = slice(first, first + ROW_TILE)
            total[rows, :] += jnp.dot(here_ref[rows, :], weight[...], preferred_element_type=jnp.float32)

    if not nearest:

        @pl.when(step == n - 1)
        def _():
            out_ref[...] = gelu(total[...])


def light_columns(place, mask, table, pieces, here, before=None):
    rows, width = here.shape
    depth, columns = width // 4, LIGHT * BLOCK
    full = pl.BlockSpec((rows, columns), lambda i, *_: (0, 0))
    nearest = before is None
    n = 3 if nearest else 2

    def block(i, place, *_):
        source = jnp.int32(0)
        last = jnp.int32(0)
        for k, (at, valid) in enumerate(light_sources(place[0], nearest)):
            last = jnp.where(valid, at, last)
            source = jnp.where(i == k, last, source)
        return 0, source

    scratch = [
        pltpu.VMEM((depth, columns), jnp.bfloat16),
        pltpu.VMEM((n * SIZE, TILE), jnp.bfloat16),
        pltpu.VMEM((2, LIGHT * depth + BLOCK, TILE), jnp.bfloat16),
        pltpu.SemaphoreType.DMA((n,)),
    ]
    if not nearest:
        scratch = [pltpu.VMEM((rows, columns), jnp.float32), *scratch, pltpu.SemaphoreType.DMA]
    any_space = pl.BlockSpec(memory_space=pl.ANY)
    return pl.pallas_call(
        functools.partial(light_kernel, nearest),
        grid_spec=pltpu.PrefetchScalarGridSpec(
            num_scalar_prefetch=3,
            grid=(n,),
            in_specs=[any_space] * len(pieces) + [pl.BlockSpec((rows, depth), block)] + ([] if nearest else [any_space]),
            out_specs=full,
            scratch_shapes=scratch,
        ),
        out_shape=jax.ShapeDtypeStruct((rows, columns), jnp.float32 if nearest else jnp.bfloat16),
        cost_estimate=BRIEF,
        compiler_params=vmem(52),
    )(place, mask, table, *pieces, here, *([] if nearest else [before]))


def product_kernel(place, *rest):
    *pieces, here_ref, end_ref, first_here, second_here, first_end, second_end, weight, sems = rest
    depth, columns = pieces[0].shape
    step = pl.program_id(0)
    half = pl.num_programs(0) // 2

    works = place[4] != 0

    @pl.when(works & (step == 0))
    def _():
        copies = []
        for i, piece in enumerate(pieces):
            rows = pl.ds(pl.multiple_of(place[i % 4] * depth, depth), depth)
            lanes = pl.ds((i // 4) * columns, columns)
            copies.append(pltpu.make_async_copy(piece, weight.at[rows, lanes], sems.at[i]))
        for copy in copies:
            copy.start()
        for copy in copies:
            copy.wait()

    def finish(preact, first_ref, second_ref):
        hidden = gelu(preact)
        first_ref[...] = hidden[:, :columns]
        second_ref[...] = hidden[:, columns:]

    @pl.when(works & (step < half))
    def _():
        finish(jnp.dot(here_ref[...], weight[...], preferred_element_type=jnp.float32), first_here, second_here)

    @pl.when(works & (step >= half))
    def _():
        parts, _, piece = end_ref.shape
        total = jnp.zeros((end_ref.shape[1], 2 * columns), jnp.float32)
        for i in range(parts):
            rows = slice(i * piece, (i + 1) * piece)
            total += jnp.dot(end_ref[i], weight[rows, :], preferred_element_type=jnp.float32)
        finish(total, first_end, second_end)


def products(place, pieces, here, end):
    columns = pieces[0].shape[1]
    rows, width = here.shape
    steps = rows // ROW_TILE
    return pl.pallas_call(
        product_kernel,
        grid_spec=pltpu.PrefetchScalarGridSpec(
            num_scalar_prefetch=1,
            grid=(2 * steps,),
            in_specs=[pl.BlockSpec(memory_space=pl.ANY)] * 8
            + [pl.BlockSpec((ROW_TILE, width), lambda i, place: (jnp.minimum(i, steps - 1) * place[4], 0))]
            + [pl.BlockSpec((end.shape[0], ROW_TILE, end.shape[2]), lambda i, place: (0, jnp.maximum(i - steps, 0) * place[4], 0))],
            out_specs=[pl.BlockSpec((ROW_TILE, columns), lambda i, place: (jnp.minimum(i, steps - 1), 0))] * 2
            + [pl.BlockSpec((ROW_TILE, columns), lambda i, place: (jnp.maximum(i - steps, 0), 0))] * 2,
            scratch_shapes=[pltpu.VMEM((width, 2 * columns), jnp.bfloat16), pltpu.SemaphoreType.DMA((8,))],
        ),
        out_shape=[jax.ShapeDtypeStruct((rows, columns), jnp.bfloat16)] * 4,
        cost_estimate=BRIEF,
        compiler_params=vmem(52),
    )(place, *pieces, here, end)


def order_kernel(table, *rest):
    *sources, out_ref, results = rest
    at = 0
    for ref in sources:
        results[:, at : at + ref.shape[1]] = ref[...]
        at += ref.shape[1]
    side = lax.broadcasted_iota(jnp.int32, (out_ref.shape[0], TILE), 1) // BLOCK
    for t in range(OWN // 2):
        values = []
        for half in range(2):
            slot = table[2 * SLOTS + 2 * t + half]
            value = results[:, pl.ds(pl.multiple_of((slot >> 1) * TILE, TILE), TILE)]
            values.append(jnp.where((slot & 1) == half, value, swap_halves(value)))
        out_ref[:, t * TILE : (t + 1) * TILE] = jnp.where(side == 0, values[0], values[1])


def in_order(table, sources):
    rows = sources[0].shape[0]
    tile = rows // 4
    widths = [s.shape[1] for s in sources]
    return pl.pallas_call(
        order_kernel,
        grid_spec=pltpu.PrefetchScalarGridSpec(
            num_scalar_prefetch=1,
            grid=(4,),
            in_specs=[pl.BlockSpec((tile, w), lambda i, table: (i, 0)) for w in widths],
            out_specs=pl.BlockSpec((tile, OWN * BLOCK), lambda i, table: (i, 0)),
            scratch_shapes=[pltpu.VMEM((tile, sum(widths)), jnp.bfloat16)],
        ),
        out_shape=jax.ShapeDtypeStruct((rows, OWN * BLOCK), jnp.bfloat16),
        cost_estimate=BRIEF,
        compiler_params=vmem(32),
    )(table, *sources)


def line_body(tokens, up_weight, block_mask):
    depth, hidden_dev = up_weight.shape
    r, c, p = (lax.axis_index(a).astype(jnp.int32) for a in ("row", "col", "rep"))
    share = hidden_dev // CORES
    rows, width = tokens.shape
    parts = CHIPS * CORES
    piece = width // parts
    place = jnp.stack([r, c, p])
    is_middle = (r == 1) | (r == 2)

    given_mask = block_mask
    block_mask = jnp.pad(block_mask, ((0, 0), (0, 1)))
    counts = block_mask.reshape(lax.axis_size("row"), -1, block_mask.shape[1]).sum(1)
    count = counts.sum(0)
    table, shared, packed, own_heavy = pack_columns(place, block_mask, count, up_weight)
    most = most_packed(counts[:, :EMPTY], count[:EMPTY], shared)

    up1, down1 = lax.ppermute(packed, "row", UP), lax.ppermute(packed, "row", DOWN)
    handed = []
    for i in range(len(SWAPS)):
        other = c ^ (i + 1)
        k = other - (other > c).astype(jnp.int32)
        handed.append(lax.dynamic_slice_in_dim(up_weight, p * share + k * SPARE * BLOCK, SPARE * BLOCK, 1))
    taken = [lax.ppermute(handed[0], "col", SWAP_X), lax.ppermute(handed[1], "col", SWAP_Y)]
    mid2 = lax.ppermute(own_heavy, "row", MIDDLE)
    up1, down1, taken = lax.optimization_barrier((up1, down1, taken))
    up2, down2 = lax.ppermute(up1, "row", UP[1:]), lax.ppermute(down1, "row", DOWN[1:])
    taken.append(lax.ppermute(after(handed[2], taken), "col", SWAP_DIAGONAL))
    light = light_columns(place, block_mask, table, [packed, up1, down1], tokens)
    mine = lax.dynamic_slice_in_dim(tokens, (c * CORES + p) * piece, piece, 1)
    mine = lax.ppermute(after(mine, packed), "row", INWARD)
    end = lax.all_gather(after(mine, up2, down2, taken[2], light), ("col", "rep"), axis=0, tiled=True)
    (first,) = whole_columns(LIGHT + HEAVY, (HEAVY,), place, block_mask, table, up_weight, taken)
    near2 = lax.ppermute(after(own_heavy, mine), "row", INWARD)
    up2, down2, first, mine = lax.optimization_barrier((up2, down2, first, mine))
    up3, down3 = lax.ppermute(up2, "row", UP[2:]), lax.ppermute(down2, "row", DOWN[2:])
    mid1 = lax.ppermute(after(first, mid2), "row", MIDDLE)
    near1 = lax.ppermute(first, "row", INWARD)
    far2 = lax.ppermute(near2, "row", MIDDLE)
    far1 = lax.ppermute(after(near1, mid1), "row", MIDDLE)
    pieces = [up2, down2, up3, down3]

    end = end.reshape(parts, rows, piece)
    at = jnp.stack([r, 3 - r, jnp.where(r <= 1, 0, 3), jnp.where(r <= 1, 3, 0), is_middle.astype(jnp.int32)])
    at = jnp.where(is_middle, at, jnp.zeros_like(at))

    weights = [first, mid1, near1, far1, own_heavy, mid2, near2, far2]
    first_here, second_here, first_end, second_end = products(at, weights, tokens, end)
    back1 = lax.ppermute(first_end, "row", OUTWARD)
    back2 = lax.ppermute(second_end, "row", OUTWARD)
    light = light_columns(place, block_mask, after(table, first_end), pieces, tokens, light)
    hidden1 = jnp.where(is_middle, after(first_here, light), back1)
    home = [lax.ppermute(hidden1, "col", pairs) for pairs in SWAPS]
    hidden2 = jnp.where(is_middle, second_here, after(back2, *home))
    return lax.cond(
        most > 2 * CAP,
        lambda table, *_: gather_body(tokens, up_weight, given_mask),
        lambda table, *results: in_order(table, results),
        table, light, hidden2, hidden1, *home,
    )


def solution(mesh):
    in_specs = (P("row", None), P("row", "col"), P())
    out_specs = P("row", ("col", "rep"))

    def body(tokens, up_weight, block_mask):
        line = dict(mesh.shape) == {"row": 4, "col": CHIPS, "rep": CORES}
        line = line and up_weight.shape[1] == CORES * OWN * BLOCK and tokens.shape[0] % (4 * ROW_TILE) in (0, 2 * ROW_TILE)
        return (line_body if line else gather_body)(tokens, up_weight, block_mask)

    return jax.shard_map(body, mesh=mesh, in_specs=in_specs, out_specs=out_specs, check_vma=False)
```

```python
import functools

import jax
import jax.numpy as jnp
from jax import lax
from jax.experimental import pallas as pl
from jax.experimental.pallas import tpu as pltpu
from jax.sharding import PartitionSpec as P

BLOCK = 64


def gather_body(tokens, up_weight, block_mask):
    weight_rows_dev, hidden_dev = up_weight.shape
    rep_count = lax.axis_size("rep")
    row_index = lax.axis_index("row")
    col_index = lax.axis_index("col")
    rep_index = lax.axis_index("rep")
    row_ids = row_index * weight_rows_dev + lax.iota(jnp.int32, weight_rows_dev)
    col_ids = col_index * hidden_dev + lax.iota(jnp.int32, hidden_dev)
    row_onehot = (
        row_ids[:, None] // BLOCK == lax.iota(jnp.int32, block_mask.shape[0])[None, :]
    ).astype(jnp.float32)
    col_onehot = (
        col_ids[:, None] // BLOCK == lax.iota(jnp.int32, block_mask.shape[1])[None, :]
    ).astype(jnp.float32)
    mask_rows = jnp.dot(row_onehot, block_mask.astype(jnp.float32), precision=lax.Precision.HIGHEST)
    local_mask = jnp.dot(mask_rows, col_onehot.T, precision=lax.Precision.HIGHEST)
    masked_weight = up_weight * local_mask.astype(jnp.bfloat16)
    share = hidden_dev // rep_count
    my_columns = lax.dynamic_slice_in_dim(masked_weight, rep_index * share, share, 1)
    preact = jnp.dot(
        tokens,
        lax.all_gather(my_columns, "row", axis=0, tiled=True),
        preferred_element_type=jnp.float32,
    )
    return jax.nn.gelu(preact, approximate=True).astype(jnp.bfloat16)


UP = [(0, 1), (1, 2), (2, 3)]
DOWN = [(3, 2), (2, 1), (1, 0)]
INWARD = [(0, 1), (3, 2)]
OUTWARD = [(1, 0), (2, 3)]
MIDDLE = [(1, 2), (2, 1)]
SWAP_X = [(0, 1), (1, 0), (2, 3), (3, 2)]
SWAP_Y = [(0, 2), (2, 0), (1, 3), (3, 1)]
SWAP_DIAGONAL = [(0, 3), (3, 0), (1, 2), (2, 1)]
SWAPS = (SWAP_X, SWAP_Y, SWAP_DIAGONAL)
SWAP_CORE = [(0, 1), (1, 0)]
CHIPS = 4
CORES = 2
OWN = 20
SPARE = 4
SLOTS = OWN + SPARE
LIGHT = 16
HEAVY = (SLOTS - LIGHT) // 2
CAP = 70
TILE = 2 * BLOCK
EMPTY = CHIPS * CORES * OWN
ROW_TILE = 384
SIZE = CAP * BLOCK
MIB = 2**20
BRIEF = pl.CostEstimate(flops=1, bytes_accessed=1, transcendentals=0)


def after(value, *earlier):
    return lax.optimization_barrier((value, *earlier))[0]


def vmem(limit):
    return pltpu.CompilerParams(vmem_limit_bytes=limit * MIB)


def swap_halves(value):
    return pltpu.roll(value.astype(jnp.float32), BLOCK, 1).astype(jnp.bfloat16)


def make_plan(count, key, table, shared, c, p, margin):
    loads = []
    for group in range(CHIPS * CORES):
        total = count[group * OWN]
        for i in range(1, OWN):
            total += count[group * OWN + i]
        loads.append(total)
    chip = [loads[2 * i] + loads[2 * i + 1] for i in range(CHIPS)]
    h, best = jnp.int32(0), chip[0]
    for i in range(1, CHIPS):
        more = chip[i] > best
        h, best = jnp.where(more, i, h), jnp.where(more, chip[i], best)
    shared[0] = h
    taken = []
    for core in range(CORES):
        mine = [loads[2 * i + core] for i in range(CHIPS)]
        heavy = sum(jnp.where(h == i, mine[i], 0) for i in range(CHIPS))

        def given(kept):
            out = []
            for i in range(CHIPS):
                spare = heavy * kept - 2 * OWN * (mine[i] + margin)
                n = sum((spare >= 2 * k * heavy).astype(jnp.int32) for k in range(1, SPARE + 1))
                out.append(jnp.where(h == i, 0, n))
            return out

        kept = lax.while_loop(
            lambda kept: 2 * (OWN - sum(given(kept))) > kept, lambda kept: kept + 1, jnp.int32(2 * (OWN - 3 * SPARE))
        )
        taken.append(given(kept))
        for i in range(CHIPS):
            shared[1 + CORES * i + core] = taken[core][i]
    taken = [jnp.where(p == 0, first, second) for first, second in zip(*taken)]
    order = [jnp.where(h <= k, taken[k + 1], taken[k]) for k in range(CHIPS - 1)]
    extra = sum(jnp.where(c == i, taken[i], 0) for i in range(CHIPS))
    base = (c * CORES + p) * OWN

    gone = []
    for i in range(OWN):
        k, j = i // SPARE, i % SPARE
        gone.append((c == h) & (j < order[k]) if k < CHIPS - 1 else jnp.bool_(False))
        key[i] = jnp.where(gone[i], -1, count[base + i])
    for q in range(SPARE):
        table[q] = EMPTY
        table[SLOTS + q] = 0
    for i in range(OWN):
        rank = jnp.int32(0)
        for j in range(OWN):
            if j != i:
                first = key[j] <= key[i] if j < i else key[j] < key[i]
                rank += first.astype(jnp.int32)
        slot = SPARE - extra + rank
        table[slot] = jnp.where(gone[i], EMPTY, base + i)
        table[SLOTS + slot] = i
        k = min(i // SPARE, CHIPS - 2)
        other = k + (h <= k).astype(jnp.int32)
        back = SLOTS + ((c ^ other) - 1) * SPARE + (SPARE - 1 - i % SPARE)
        table[2 * SLOTS + i] = jnp.where(gone[i], back, slot)
    k = c - (c > h).astype(jnp.int32)
    for i in range(SPARE):

        @pl.when(i < extra)
        def _():
            table[SLOTS - 1 - i] = (h * CORES + p) * OWN + SPARE * k + i
            table[2 * SLOTS - 1 - i] = OWN + i

    table[2 * SLOTS + OWN] = c ^ h


TABLE = 2 * SLOTS + OWN + 1


def pack_kernel(place, mask, count, w_ref, table, shared, packed, own_heavy, key, both, line):
    r, c, p = place[0], place[1], place[2]
    make_plan(count, key, table, shared, c, p, 3 * mask.shape[0] // 2)
    row_blocks = w_ref.shape[0] // BLOCK
    for t in range(w_ref.shape[1] // TILE):
        value = w_ref[:, t * TILE : (t + 1) * TILE]
        both[0, :, t * TILE : (t + 1) * TILE] = value
        both[1, :, t * TILE : (t + 1) * TILE] = swap_halves(value)
    side = lax.broadcasted_iota(jnp.int32, (BLOCK, TILE), 1) // BLOCK

    def lanes(source):
        return pl.ds(pl.multiple_of((source >> 1) * TILE, TILE), TILE)

    def column(q, s):
        col = table[q]
        source = table[SLOTS + q]
        for i in range(row_blocks):
            at = jnp.minimum(s, 2 * CAP)
            value = both[(source ^ at) & 1, i * BLOCK : (i + 1) * BLOCK, lanes(source)]
            line[pl.ds(pl.multiple_of(at * BLOCK, BLOCK), BLOCK), :] = value
            s = s + mask[r * row_blocks + i, col]
        return s

    lax.fori_loop(0, LIGHT, column, jnp.int32(0))
    for n in range(CAP):
        left = line[2 * n * BLOCK : (2 * n + 1) * BLOCK, :]
        right = line[(2 * n + 1) * BLOCK : (2 * n + 2) * BLOCK, :]
        packed[n * BLOCK : (n + 1) * BLOCK, :] = jnp.where(side == 0, left, right)

    for t in range(HEAVY // 2):
        slots = (LIGHT + 2 * t, LIGHT + 2 * t + 1)

        def block(i, _):
            rows = pl.ds(pl.multiple_of(i * BLOCK, BLOCK), BLOCK)
            values = []
            for half in range(2):
                source, col = table[SLOTS + slots[half]], table[slots[half]]
                value = both[(source & 1) ^ half, rows, lanes(source)]
                values.append(jnp.where(mask[r * row_blocks + i, col] != 0, value, jnp.zeros_like(value)))
            own_heavy[rows, t * TILE : (t + 1) * TILE] = jnp.where(side == 0, values[0], values[1])
            return 0

        lax.fori_loop(0, row_blocks, block, 0)


def pack_columns(place, mask, count, weight):
    depth, share = weight.shape[0], OWN * BLOCK
    smem = pl.BlockSpec(memory_space=pltpu.SMEM)
    return pl.pallas_call(
        pack_kernel,
        grid_spec=pltpu.PrefetchScalarGridSpec(
            num_scalar_prefetch=3,
            grid=(1,),
            in_specs=[pl.BlockSpec((depth, share), lambda i, place, mask, count: (0, place[2]))],
            out_specs=[
                smem,
                smem,
                pl.BlockSpec((CAP * BLOCK, TILE), lambda i, place, mask, count: (0, 0)),
                pl.BlockSpec((depth, HEAVY * BLOCK), lambda i, place, mask, count: (0, 0)),
            ],
            scratch_shapes=[
                pltpu.SMEM((OWN,), jnp.int32),
                pltpu.VMEM((2, depth, share), jnp.bfloat16),
                pltpu.VMEM((2 * SIZE + BLOCK, TILE), jnp.bfloat16),
            ],
        ),
        out_shape=[
            jax.ShapeDtypeStruct((TABLE,), jnp.int32),
            jax.ShapeDtypeStruct((1 + CHIPS * CORES,), jnp.int32),
            jax.ShapeDtypeStruct((CAP * BLOCK, TILE), jnp.bfloat16),
            jax.ShapeDtypeStruct((depth, HEAVY * BLOCK), jnp.bfloat16),
        ],
        cost_estimate=BRIEF,
        compiler_params=vmem(48),
    )(place, mask, count, weight)


def most_packed(counts, count, shared):
    groups = CHIPS * CORES
    column = lax.iota(jnp.int32, groups * OWN)
    group, i = column // OWN, column % OWN
    h, taken = shared[0], shared[1 : 1 + groups]
    to = i // SPARE + (h <= i // SPARE).astype(jnp.int32)
    ways = jnp.sum(jnp.where((to * CORES + group % CORES)[:, None] == lax.iota(jnp.int32, groups), taken, 0), 1)
    gone = (group // CORES == h) & (i < 3 * SPARE) & (i % SPARE < ways)
    key = jnp.where(gone, -1, count)
    before = (key[None, :] < key[:, None]) | ((key[None, :] == key[:, None]) & (column[None, :] < column[:, None]))
    rank = jnp.sum((before & (group[None, :] == group[:, None])).astype(jnp.int32), 1)
    extra = jnp.sum(jnp.where(group[:, None] == lax.iota(jnp.int32, groups), taken, 0), 1)
    light = (SPARE - extra + rank < LIGHT) & ~gone
    return jnp.max(jnp.sum(jnp.where(light, counts, 0).reshape(counts.shape[0], groups, OWN), 2))


def whole_kernel(first, place, mask, table, w_ref, x_ref, y_ref, d_ref, *rest):
    *outs, taken = rest
    r = place[0]
    row_blocks = w_ref.shape[0] // BLOCK
    side = lax.broadcasted_iota(jnp.int32, (BLOCK, TILE), 1) // BLOCK
    for i, ref in enumerate((x_ref, y_ref, d_ref)):

        @pl.when(table[2 * SLOTS + OWN] == i + 1)
        def _():
            taken[...] = ref[...]

    slot = first
    for out in outs:
        for t in range(out.shape[1] // TILE):
            halves = []
            for half in range(2):
                source, col = table[SLOTS + slot], table[slot]
                slot += 1
                own = jnp.minimum(source, OWN - 1)
                other = jnp.maximum(source - OWN, 0)
                halves.append((
                    source >= OWN, col, (source & 1) != half,
                    pl.ds(pl.multiple_of((own >> 1) * TILE, TILE), TILE),
                    pl.ds(pl.multiple_of((other >> 1) * TILE, TILE), TILE),
                ))

            def block(i, _):
                rows = pl.ds(pl.multiple_of(i * BLOCK, BLOCK), BLOCK)
                values = []
                for is_taken, col, swap, own, other in halves:
                    value = jnp.where(is_taken, taken[rows, other], w_ref[rows, own])
                    value = jnp.where(swap, swap_halves(value), value)
                    values.append(jnp.where(mask[r * row_blocks + i, col] != 0, value, jnp.zeros_like(value)))
                out[rows, t * TILE : (t + 1) * TILE] = jnp.where(side == 0, values[0], values[1])
                return 0

            lax.fori_loop(0, row_blocks, block, 0)


def whole_columns(first, widths, place, mask, table, weight, taken):
    rows, width = weight.shape[0], OWN * BLOCK
    full = lambda shape: pl.BlockSpec(shape, lambda i, place, mask, table: (0, 0))
    return pl.pallas_call(
        functools.partial(whole_kernel, first),
        grid_spec=pltpu.PrefetchScalarGridSpec(
            num_scalar_prefetch=3,
            grid=(1,),
            in_specs=[pl.BlockSpec((rows, width), lambda i, place, mask, table: (0, place[2]))]
            + [full(taken[0].shape)] * 3,
            out_specs=[full((rows, w * BLOCK)) for w in widths],
            scratch_shapes=[pltpu.VMEM(taken[0].shape, jnp.bfloat16)],
        ),
        out_shape=[jax.ShapeDtypeStruct((rows, w * BLOCK), jnp.bfloat16) for w in widths],
        cost_estimate=BRIEF,
        compiler_params=vmem(48),
    )(place, mask, table, weight, *taken)


def gelu(preact):
    return jax.nn.gelu(preact, approximate=True).astype(jnp.bfloat16)


def light_sources(me, mode):
    if mode == "near":
        return [(me, me >= 0), (me - 1, me >= 1), (me + 1, me <= 2)]
    side = jnp.where(me <= 1, 1, -1)
    middle = (me == 1) | (me == 2)
    return [(me + 2 * side, me >= 0), (me + 3 * side, ~middle)]


def light_kernel(mode, place, mask, table, *rest):
    nearest = mode == "near"
    n = 3 if nearest else 2
    pieces, rest = rest[: n if nearest else 2 * n], rest[n if nearest else 2 * n :]
    if nearest:
        here_ref, total, weight, blocks, lines, sems = rest
    else:
        here_ref, before, out_ref, total, weight, blocks, lines, sems, before_sem = rest
        load = pltpu.make_async_copy(before, total, before_sem)
    step = pl.program_id(0)
    row_blocks = weight.shape[0] // BLOCK
    zero = lines.shape[1] - BLOCK
    me = place[0]
    sources = light_sources(me, mode)

    def copies(i):
        slot = blocks.at[pl.ds(i * SIZE, SIZE)]
        if nearest:
            return [(sources[i][1], pltpu.make_async_copy(pieces[i], slot, sems.at[i]))]
        return [
            (sources[i][1] & (me <= 1 if k else me > 1), pltpu.make_async_copy(pieces[2 * i + k], slot, sems.at[i]))
            for k in range(2)
        ]

    @pl.when(step == 0)
    def _():
        for i in range(n):
            for there, copy in copies(i):
                pl.when(there)(copy.start)
        for half in range(2):
            lines[half, zero : zero + BLOCK, :] = jnp.zeros((BLOCK, TILE), jnp.bfloat16)
        if nearest:
            total[...] = jnp.zeros_like(total)
        else:
            load.start()

    for i in range(n):
        for there, copy in copies(i):
            pl.when((step == i) & there)(copy.wait)

    source, valid = sources[0]
    for i in range(1, n):
        source = jnp.where(step == i, sources[i][0], source)
        valid = jnp.where(step == i, sources[i][1], valid)

    @pl.when(valid)
    def _():
        side = lax.broadcasted_iota(jnp.int32, (BLOCK, TILE), 1) // BLOCK
        many = 10

        def spread(t, _):
            value = blocks[pl.ds(pl.multiple_of(step * SIZE + t * many * BLOCK, BLOCK), many * BLOCK), :]
            other = swap_halves(value)
            for k in range(many):
                first = pl.ds(pl.multiple_of(2 * (t * many + k) * BLOCK, BLOCK), BLOCK)
                second = pl.ds(pl.multiple_of(2 * (t * many + k) * BLOCK + BLOCK, BLOCK), BLOCK)
                rows = slice(k * BLOCK, (k + 1) * BLOCK)
                lines[0, first, :] = value[rows]
                lines[1, first, :] = other[rows]
                lines[0, second, :] = other[rows]
                lines[1, second, :] = value[rows]
            return 0

        lax.fori_loop(0, CAP // many, spread, 0)

        def pair(t, row):
            cols = [table[2 * t], table[2 * t + 1]]
            kept = [[mask[source * row_blocks + i, col] * BLOCK for i in range(row_blocks)] for col in cols]
            at = [row, row + sum(kept[0])]
            lanes = pl.ds(pl.multiple_of(t * TILE, TILE), TILE)
            for i in range(row_blocks):
                values = []
                for half in range(2):
                    rows = pl.multiple_of(jnp.where(kept[half][i] != 0, at[half], zero), BLOCK)
                    values.append(lines[half, pl.ds(rows, BLOCK), :])
                    at[half] = at[half] + kept[half][i]
                weight[i * BLOCK : (i + 1) * BLOCK, lanes] = jnp.where(side == 0, values[0], values[1])
            return at[1]

        lax.fori_loop(0, LIGHT // 2, pair, jnp.int32(0))
        if not nearest:
            pl.when(step == 0)(load.wait)
        for first in range(0, total.shape[0], ROW_TILE):
            rows = slice(first, first + ROW_TILE)
            total[rows, :] += jnp.dot(here_ref[rows, :], weight[...], preferred_element_type=jnp.float32)

    if not nearest:

        @pl.when(step == n - 1)
        def _():
            out_ref[...] = gelu(total[...])


def light_columns(mode, place, mask, table, pieces, here, before=None):
    rows, width = here.shape
    depth, columns = width // 4, LIGHT * BLOCK
    full = pl.BlockSpec((rows, columns), lambda i, *_: (0, 0))
    nearest = mode == "near"
    n = 3 if nearest else 2

    def block(i, place, *_):
        source = jnp.int32(0)
        last = jnp.int32(0)
        for k, (at, valid) in enumerate(light_sources(place[0], mode)):
            last = jnp.where(valid, at, last)
            source = jnp.where(i == k, last, source)
        return 0, source

    scratch = [
        pltpu.VMEM((depth, columns), jnp.bfloat16),
        pltpu.VMEM((n * SIZE, TILE), jnp.bfloat16),
        pltpu.VMEM((2, LIGHT * depth + BLOCK, TILE), jnp.bfloat16),
        pltpu.SemaphoreType.DMA((n,)),
    ]
    if not nearest:
        scratch = [pltpu.VMEM((rows, columns), jnp.float32), *scratch, pltpu.SemaphoreType.DMA]
    any_space = pl.BlockSpec(memory_space=pl.ANY)
    return pl.pallas_call(
        functools.partial(light_kernel, mode),
        grid_spec=pltpu.PrefetchScalarGridSpec(
            num_scalar_prefetch=3,
            grid=(n,),
            in_specs=[any_space] * len(pieces) + [pl.BlockSpec((rows, depth), block)] + ([] if nearest else [any_space]),
            out_specs=full,
            scratch_shapes=scratch,
        ),
        out_shape=jax.ShapeDtypeStruct((rows, columns), jnp.float32 if nearest else jnp.bfloat16),
        cost_estimate=BRIEF,
        compiler_params=vmem(52),
    )(place, mask, table, *pieces, here, *([] if nearest else [before]))


def early_kernel(place, *rest):
    *pieces, tokens_ref, total1, total2, weight, sems = rest
    columns = pieces[0].shape[1]
    step = pl.program_id(0)
    works = place[4] != 0
    copies = [
        pltpu.make_async_copy(piece, weight.at[i % 3, :, pl.ds((i // 3) * columns, columns)], sems.at[i])
        for i, piece in enumerate(pieces)
    ]

    @pl.when(works & (step == 0))
    def _():
        for copy in copies:
            copy.start()

    for k in range(3):

        @pl.when(works & (step == k))
        def _():
            copies[k].wait()
            if k < 2:
                copies[3 + k].wait()
            for first in range(0, total1.shape[0], ROW_TILE):
                rows = slice(first, first + ROW_TILE)
                here = tokens_ref.at[rows, :] if len(tokens_ref.shape) == 2 else tokens_ref.at[:, rows, :]
                value = tokens_dot(here, weight.at[k] if k < 2 else weight.at[k, :, :columns])
                if k == 0:
                    total1[rows, :] = value[:, :columns]
                    total2[rows, :] = value[:, columns:]
                else:
                    total1[rows, :] += value[:, :columns]
                    if k < 2:
                        total2[rows, :] += value[:, columns:]


def tokens_dot(tokens_ref, weight):
    if len(tokens_ref.shape) == 2:
        return jnp.dot(tokens_ref[...], weight[...], preferred_element_type=jnp.float32)
    parts, _, piece = tokens_ref.shape
    dots = [
        jnp.dot(tokens_ref[i], weight[i * piece : (i + 1) * piece, :], preferred_element_type=jnp.float32)
        for i in range(parts)
    ]
    return sum(dots[1:], dots[0])


def tokens_block(tokens, depth, rows, at):
    if tokens.ndim == 2:
        return pl.BlockSpec((rows, depth), lambda i, place: (at(i, place)[0], at(i, place)[1]))
    parts = depth // tokens.shape[2]
    return pl.BlockSpec((parts, rows, tokens.shape[2]), lambda i, place: (at(i, place)[1], at(i, place)[0], 0))


def early_products(place, pieces, tokens):
    depth, columns = pieces[0].shape
    rows = tokens.shape[-2]

    def at(i, place):
        return 0, jnp.where(i == 0, place[0], jnp.where(i == 1, place[1], place[2]))

    return pl.pallas_call(
        early_kernel,
        grid_spec=pltpu.PrefetchScalarGridSpec(
            num_scalar_prefetch=1,
            grid=(3,),
            in_specs=[pl.BlockSpec(memory_space=pl.ANY)] * 5 + [tokens_block(tokens, depth, rows, at)],
            out_specs=[pl.BlockSpec((rows, columns), lambda i, place: (0, 0))] * 2,
            scratch_shapes=[pltpu.VMEM((3, depth, 2 * columns), jnp.bfloat16), pltpu.SemaphoreType.DMA((5,))],
        ),
        out_shape=[jax.ShapeDtypeStruct((rows, columns), jnp.float32)] * 2,
        cost_estimate=BRIEF,
        compiler_params=vmem(48),
    )(place, *pieces, tokens)


def last_kernel(n, place, *rest):
    pieces, here_refs, end_refs, rest = rest[:n], rest[n : 2 * n], rest[2 * n : 3 * n], rest[3 * n :]
    here_total, end_total, out_here, out_end, weight, sems = rest
    step = pl.program_id(0)
    half = pl.num_programs(0) // 2
    works = place[4] != 0

    @pl.when(works & (step == 0))
    def _():
        copies = [pltpu.make_async_copy(piece, weight.at[i], sems.at[i]) for i, piece in enumerate(pieces)]
        for copy in copies:
            copy.start()
        for copy in copies:
            copy.wait()

    def finish(refs, total, out_ref):
        preact = total[...]
        for i, ref in enumerate(refs):
            preact += tokens_dot(ref, weight.at[i])
        out_ref[...] = gelu(preact)

    pl.when(works & (step < half))(lambda: finish(here_refs, here_total, out_here))
    pl.when(works & (step >= half))(lambda: finish(end_refs, end_total, out_end))


def last_products(place, pieces, here, end, here_total, end_total):
    n = len(pieces)
    depth, columns = pieces[0].shape
    rows = here.shape[0]
    steps = rows // ROW_TILE
    here_at = lambda k: lambda i, place: (jnp.minimum(i, steps - 1) * place[4], place[k])
    end_at = lambda k: lambda i, place: (jnp.maximum(i - steps, 0) * place[4], place[k])
    total = lambda at: pl.BlockSpec((ROW_TILE, columns), lambda i, place: (at(i, place)[0], 0))
    ks = range(4 - n, 4)
    return pl.pallas_call(
        functools.partial(last_kernel, n),
        grid_spec=pltpu.PrefetchScalarGridSpec(
            num_scalar_prefetch=1,
            grid=(2 * steps,),
            in_specs=[pl.BlockSpec(memory_space=pl.ANY)] * n
            + [tokens_block(here, depth, ROW_TILE, here_at(k)) for k in ks]
            + [tokens_block(end, depth, ROW_TILE, end_at(k)) for k in ks]
            + [total(here_at(3)), total(end_at(3))],
            out_specs=[
                pl.BlockSpec((ROW_TILE, columns), lambda i, place: (jnp.minimum(i, steps - 1), 0)),
                pl.BlockSpec((ROW_TILE, columns), lambda i, place: (jnp.maximum(i - steps, 0), 0)),
            ],
            scratch_shapes=[pltpu.VMEM((n, depth, columns), jnp.bfloat16), pltpu.SemaphoreType.DMA((n,))],
        ),
        out_shape=[jax.ShapeDtypeStruct((rows, columns), jnp.bfloat16)] * 2,
        cost_estimate=BRIEF,
        compiler_params=vmem(48),
    )(place, *pieces, *[here] * n, *[end] * n, here_total, end_total)


def order_kernel(table, place, light, second_here, second_back, *rest):
    *sources, out_ref, results = rest
    at = light.shape[1] + second_here.shape[1]
    results[:, : light.shape[1]] = light[...]

    @pl.when(place[4] != 0)
    def _():
        results[:, light.shape[1] : at] = second_here[...]

    @pl.when(place[4] == 0)
    def _():
        results[:, light.shape[1] : at] = second_back[...]

    for ref in sources:
        results[:, at : at + ref.shape[1]] = ref[...]
        at += ref.shape[1]
    side = lax.broadcasted_iota(jnp.int32, (out_ref.shape[0], TILE), 1) // BLOCK
    for t in range(OWN // 2):
        values = []
        for half in range(2):
            slot = table[2 * SLOTS + 2 * t + half]
            value = results[:, pl.ds(pl.multiple_of((slot >> 1) * TILE, TILE), TILE)]
            values.append(jnp.where((slot & 1) == half, value, swap_halves(value)))
        out_ref[:, t * TILE : (t + 1) * TILE] = jnp.where(side == 0, values[0], values[1])


def in_order(table, place, sources):
    rows = sources[0].shape[0]
    tile = rows // 4
    widths = [s.shape[1] for s in sources]
    wide = sum(widths) - widths[1]
    return pl.pallas_call(
        order_kernel,
        grid_spec=pltpu.PrefetchScalarGridSpec(
            num_scalar_prefetch=2,
            grid=(4,),
            in_specs=[pl.BlockSpec((tile, w), lambda i, *_: (i, 0)) for w in widths],
            out_specs=pl.BlockSpec((tile, OWN * BLOCK), lambda i, *_: (i, 0)),
            scratch_shapes=[pltpu.VMEM((tile, wide), jnp.bfloat16)],
        ),
        out_shape=jax.ShapeDtypeStruct((rows, OWN * BLOCK), jnp.bfloat16),
        cost_estimate=BRIEF,
        compiler_params=vmem(32),
    )(table, place, *sources)


def line_body(tokens, up_weight, block_mask):
    depth, hidden_dev = up_weight.shape
    r, c, p = (lax.axis_index(a).astype(jnp.int32) for a in ("row", "col", "rep"))
    share = hidden_dev // CORES
    rows, width = tokens.shape
    parts = CHIPS * CORES
    piece = width // parts
    place = jnp.stack([r, c, p])
    is_middle = (r == 1) | (r == 2)

    given_mask = block_mask
    block_mask = jnp.pad(block_mask, ((0, 0), (0, 1)))
    counts = block_mask.reshape(lax.axis_size("row"), -1, block_mask.shape[1]).sum(1)
    count = counts.sum(0)
    table, shared, packed, own_heavy = pack_columns(place, block_mask, count, up_weight)
    most = most_packed(counts[:, :EMPTY], count[:EMPTY], shared)

    up1, down1 = lax.ppermute(packed, "row", UP), lax.ppermute(packed, "row", DOWN)
    handed = []
    for i in range(len(SWAPS)):
        other = c ^ (i + 1)
        k = other - (other > c).astype(jnp.int32)
        handed.append(lax.dynamic_slice_in_dim(up_weight, p * share + k * SPARE * BLOCK, SPARE * BLOCK, 1))
    taken = [lax.ppermute(handed[0], "col", SWAP_X), lax.ppermute(handed[1], "col", SWAP_Y)]
    mid2 = lax.ppermute(own_heavy, "row", MIDDLE)
    up1, down1, taken = lax.optimization_barrier((up1, down1, taken))
    up2, down2 = lax.ppermute(up1, "row", UP[1:]), lax.ppermute(down1, "row", DOWN[1:])
    taken.append(lax.ppermute(after(handed[2], taken), "col", SWAP_DIAGONAL))
    light = light_columns("near", place, block_mask, table, [packed, up1, down1], tokens)
    mine = lax.dynamic_slice_in_dim(tokens, (c * CORES + p) * piece, piece, 1)
    mine = lax.ppermute(after(mine, packed), "row", INWARD)
    end = lax.all_gather(after(mine, up2, down2, taken[2], light), ("col", "rep"), axis=0, tiled=True)
    (first,) = whole_columns(LIGHT + HEAVY, (HEAVY,), place, block_mask, table, up_weight, taken)
    near2 = lax.ppermute(after(own_heavy, mine, first), "row", INWARD)
    up2, down2, first, mine = lax.optimization_barrier((up2, down2, first, mine))
    up3, down3 = lax.ppermute(up2, "row", UP[2:]), lax.ppermute(down2, "row", DOWN[2:])
    mid1 = lax.ppermute(after(first, mid2), "row", MIDDLE)
    near1 = lax.ppermute(first, "row", INWARD)
    far1 = lax.ppermute(near1, "row", MIDDLE)
    at = jnp.stack([r, 3 - r, jnp.where(r <= 1, 0, 3), jnp.where(r <= 1, 3, 0), is_middle.astype(jnp.int32)])
    at = jnp.where(is_middle, at, jnp.zeros_like(at))
    early = [first, mid1, near1, own_heavy, mid2]
    here_total1, here_total2 = early_products(at, early, tokens)
    far2 = lax.ppermute(after(near2, near1, here_total1, up3, down3), "row", MIDDLE)
    pieces = [up2, down2, up3, down3]

    end = end.reshape(parts, rows, piece)
    end_total1, end_total2 = early_products(at, early, after(end, here_total1))
    first_here, first_end = last_products(at, [far1], tokens, end, here_total1, end_total1)
    back1 = lax.ppermute(first_end, "row", OUTWARD)
    far2 = after(far2, first_end)
    second_here, second_end = last_products(at, [near2, far2], tokens, end, here_total2, end_total2)
    back2 = lax.ppermute(second_end, "row", OUTWARD)
    hidden1 = jnp.where(is_middle, after(first_here, second_here), back1)
    home = [lax.ppermute(hidden1, "col", pairs) for pairs in SWAPS]
    light = light_columns("rest", place, block_mask, after(table, hidden1), pieces, tokens, light)
    results = [light, second_here, after(back2, *home), hidden1, *home]
    return lax.cond(
        most > 2 * CAP,
        lambda *_: gather_body(tokens, up_weight, given_mask),
        lambda table, *results: in_order(table, at, results),
        table, *results,
    )


def solution(mesh):
    in_specs = (P("row", None), P("row", "col"), P())
    out_specs = P("row", ("col", "rep"))

    def body(tokens, up_weight, block_mask):
        line = dict(mesh.shape) == {"row": 4, "col": CHIPS, "rep": CORES}
        line = line and up_weight.shape[1] == CORES * OWN * BLOCK and tokens.shape[0] % (4 * ROW_TILE) in (0, 2 * ROW_TILE)
        return (line_body if line else gather_body)(tokens, up_weight, block_mask)

    return jax.shard_map(body, mesh=mesh, in_specs=in_specs, out_specs=out_specs, check_vma=False)
```

```python
import functools

import jax
import jax.numpy as jnp
from jax import lax
from jax.experimental import pallas as pl
from jax.experimental.pallas import tpu as pltpu
from jax.sharding import PartitionSpec as P

BLOCK = 64


def gather_body(tokens, up_weight, block_mask):
    weight_rows_dev, hidden_dev = up_weight.shape
    rep_count = lax.axis_size("rep")
    row_index = lax.axis_index("row")
    col_index = lax.axis_index("col")
    rep_index = lax.axis_index("rep")
    row_ids = row_index * weight_rows_dev + lax.iota(jnp.int32, weight_rows_dev)
    col_ids = col_index * hidden_dev + lax.iota(jnp.int32, hidden_dev)
    row_onehot = (
        row_ids[:, None] // BLOCK == lax.iota(jnp.int32, block_mask.shape[0])[None, :]
    ).astype(jnp.float32)
    col_onehot = (
        col_ids[:, None] // BLOCK == lax.iota(jnp.int32, block_mask.shape[1])[None, :]
    ).astype(jnp.float32)
    mask_rows = jnp.dot(row_onehot, block_mask.astype(jnp.float32), precision=lax.Precision.HIGHEST)
    local_mask = jnp.dot(mask_rows, col_onehot.T, precision=lax.Precision.HIGHEST)
    masked_weight = up_weight * local_mask.astype(jnp.bfloat16)
    share = hidden_dev // rep_count
    my_columns = lax.dynamic_slice_in_dim(masked_weight, rep_index * share, share, 1)
    preact = jnp.dot(
        tokens,
        lax.all_gather(my_columns, "row", axis=0, tiled=True),
        preferred_element_type=jnp.float32,
    )
    return jax.nn.gelu(preact, approximate=True).astype(jnp.bfloat16)


UP = [(0, 1), (1, 2), (2, 3)]
DOWN = [(3, 2), (2, 1), (1, 0)]
INWARD = [(0, 1), (3, 2)]
OUTWARD = [(1, 0), (2, 3)]
MIDDLE = [(1, 2), (2, 1)]
SWAP_X = [(0, 1), (1, 0), (2, 3), (3, 2)]
SWAP_Y = [(0, 2), (2, 0), (1, 3), (3, 1)]
SWAP_DIAGONAL = [(0, 3), (3, 0), (1, 2), (2, 1)]
SWAPS = (SWAP_X, SWAP_Y, SWAP_DIAGONAL)
SWAP_CORE = [(0, 1), (1, 0)]
CHIPS = 4
CORES = 2
OWN = 20
SPARE = 4
SLOTS = OWN + SPARE
LIGHT = 16
HEAVY = (SLOTS - LIGHT) // 2
CAP = 70
TILE = 2 * BLOCK
EMPTY = CHIPS * CORES * OWN
ROW_TILE = 384
SIZE = CAP * BLOCK
MIB = 2**20
BRIEF = pl.CostEstimate(flops=1, bytes_accessed=1, transcendentals=0)


def after(value, *earlier):
    return lax.optimization_barrier((value, *earlier))[0]


def vmem(limit):
    return pltpu.CompilerParams(vmem_limit_bytes=limit * MIB)


def swap_halves(value):
    return pltpu.roll(value.astype(jnp.float32), BLOCK, 1).astype(jnp.bfloat16)


def make_plan(count, key, table, shared, c, p, margin):
    loads = []
    for group in range(CHIPS * CORES):
        total = count[group * OWN]
        for i in range(1, OWN):
            total += count[group * OWN + i]
        loads.append(total)
    chip = [loads[2 * i] + loads[2 * i + 1] for i in range(CHIPS)]
    h, best = jnp.int32(0), chip[0]
    for i in range(1, CHIPS):
        more = chip[i] > best
        h, best = jnp.where(more, i, h), jnp.where(more, chip[i], best)
    shared[0] = h
    taken = []
    for core in range(CORES):
        mine = [loads[2 * i + core] for i in range(CHIPS)]
        heavy = sum(jnp.where(h == i, mine[i], 0) for i in range(CHIPS))

        def given(kept):
            out = []
            for i in range(CHIPS):
                spare = heavy * kept - 2 * OWN * (mine[i] + margin)
                n = sum((spare >= 2 * k * heavy).astype(jnp.int32) for k in range(1, SPARE + 1))
                out.append(jnp.where(h == i, 0, n))
            return out

        kept = lax.while_loop(
            lambda kept: 2 * (OWN - sum(given(kept))) > kept, lambda kept: kept + 1, jnp.int32(2 * (OWN - 3 * SPARE))
        )
        taken.append(given(kept))
        for i in range(CHIPS):
            shared[1 + CORES * i + core] = taken[core][i]
    taken = [jnp.where(p == 0, first, second) for first, second in zip(*taken)]
    order = [jnp.where(h <= k, taken[k + 1], taken[k]) for k in range(CHIPS - 1)]
    extra = sum(jnp.where(c == i, taken[i], 0) for i in range(CHIPS))
    base = (c * CORES + p) * OWN

    gone = []
    for i in range(OWN):
        k, j = i // SPARE, i % SPARE
        gone.append((c == h) & (j < order[k]) if k < CHIPS - 1 else jnp.bool_(False))
        key[i] = jnp.where(gone[i], -1, count[base + i])
    for q in range(SPARE):
        table[q] = EMPTY
        table[SLOTS + q] = 0
    for i in range(OWN):
        rank = jnp.int32(0)
        for j in range(OWN):
            if j != i:
                first = key[j] <= key[i] if j < i else key[j] < key[i]
                rank += first.astype(jnp.int32)
        slot = SPARE - extra + rank
        table[slot] = jnp.where(gone[i], EMPTY, base + i)
        table[SLOTS + slot] = i
        k = min(i // SPARE, CHIPS - 2)
        other = k + (h <= k).astype(jnp.int32)
        back = SLOTS + ((c ^ other) - 1) * SPARE + (SPARE - 1 - i % SPARE)
        table[2 * SLOTS + i] = jnp.where(gone[i], back, slot)
    k = c - (c > h).astype(jnp.int32)
    for i in range(SPARE):

        @pl.when(i < extra)
        def _():
            table[SLOTS - 1 - i] = (h * CORES + p) * OWN + SPARE * k + i
            table[2 * SLOTS - 1 - i] = OWN + i

    table[2 * SLOTS + OWN] = c ^ h


TABLE = 2 * SLOTS + OWN + 1


def pack_kernel(place, mask, count, w_ref, table, shared, packed, own_heavy, key, both, line):
    r, c, p = place[0], place[1], place[2]
    make_plan(count, key, table, shared, c, p, 3 * mask.shape[0] // 2)
    row_blocks = w_ref.shape[0] // BLOCK
    for t in range(w_ref.shape[1] // TILE):
        value = w_ref[:, t * TILE : (t + 1) * TILE]
        both[0, :, t * TILE : (t + 1) * TILE] = value
        both[1, :, t * TILE : (t + 1) * TILE] = swap_halves(value)
    side = lax.broadcasted_iota(jnp.int32, (BLOCK, TILE), 1) // BLOCK

    def lanes(source):
        return pl.ds(pl.multiple_of((source >> 1) * TILE, TILE), TILE)

    def column(q, s):
        col = table[q]
        source = table[SLOTS + q]
        for i in range(row_blocks):
            at = jnp.minimum(s, 2 * CAP)
            value = both[(source ^ at) & 1, i * BLOCK : (i + 1) * BLOCK, lanes(source)]
            line[pl.ds(pl.multiple_of(at * BLOCK, BLOCK), BLOCK), :] = value
            s = s + mask[r * row_blocks + i, col]
        return s

    lax.fori_loop(0, LIGHT, column, jnp.int32(0))
    for n in range(CAP):
        left = line[2 * n * BLOCK : (2 * n + 1) * BLOCK, :]
        right = line[(2 * n + 1) * BLOCK : (2 * n + 2) * BLOCK, :]
        packed[n * BLOCK : (n + 1) * BLOCK, :] = jnp.where(side == 0, left, right)

    for t in range(HEAVY // 2):
        slots = (LIGHT + 2 * t, LIGHT + 2 * t + 1)

        def block(i, _):
            rows = pl.ds(pl.multiple_of(i * BLOCK, BLOCK), BLOCK)
            values = []
            for half in range(2):
                source, col = table[SLOTS + slots[half]], table[slots[half]]
                value = both[(source & 1) ^ half, rows, lanes(source)]
                values.append(jnp.where(mask[r * row_blocks + i, col] != 0, value, jnp.zeros_like(value)))
            own_heavy[rows, t * TILE : (t + 1) * TILE] = jnp.where(side == 0, values[0], values[1])
            return 0

        lax.fori_loop(0, row_blocks, block, 0)


def pack_columns(place, mask, count, weight):
    depth, share = weight.shape[0], OWN * BLOCK
    smem = pl.BlockSpec(memory_space=pltpu.SMEM)
    return pl.pallas_call(
        pack_kernel,
        grid_spec=pltpu.PrefetchScalarGridSpec(
            num_scalar_prefetch=3,
            grid=(1,),
            in_specs=[pl.BlockSpec((depth, share), lambda i, place, mask, count: (0, place[2]))],
            out_specs=[
                smem,
                smem,
                pl.BlockSpec((CAP * BLOCK, TILE), lambda i, place, mask, count: (0, 0)),
                pl.BlockSpec((depth, HEAVY * BLOCK), lambda i, place, mask, count: (0, 0)),
            ],
            scratch_shapes=[
                pltpu.SMEM((OWN,), jnp.int32),
                pltpu.VMEM((2, depth, share), jnp.bfloat16),
                pltpu.VMEM((2 * SIZE + BLOCK, TILE), jnp.bfloat16),
            ],
        ),
        out_shape=[
            jax.ShapeDtypeStruct((TABLE,), jnp.int32),
            jax.ShapeDtypeStruct((1 + CHIPS * CORES,), jnp.int32),
            jax.ShapeDtypeStruct((CAP * BLOCK, TILE), jnp.bfloat16),
            jax.ShapeDtypeStruct((depth, HEAVY * BLOCK), jnp.bfloat16),
        ],
        cost_estimate=BRIEF,
        compiler_params=vmem(48),
    )(place, mask, count, weight)


def most_packed(counts, count, shared):
    groups = CHIPS * CORES
    column = lax.iota(jnp.int32, groups * OWN)
    group, i = column // OWN, column % OWN
    h, taken = shared[0], shared[1 : 1 + groups]
    to = i // SPARE + (h <= i // SPARE).astype(jnp.int32)
    ways = jnp.sum(jnp.where((to * CORES + group % CORES)[:, None] == lax.iota(jnp.int32, groups), taken, 0), 1)
    gone = (group // CORES == h) & (i < 3 * SPARE) & (i % SPARE < ways)
    key = jnp.where(gone, -1, count)
    before = (key[None, :] < key[:, None]) | ((key[None, :] == key[:, None]) & (column[None, :] < column[:, None]))
    rank = jnp.sum((before & (group[None, :] == group[:, None])).astype(jnp.int32), 1)
    extra = jnp.sum(jnp.where(group[:, None] == lax.iota(jnp.int32, groups), taken, 0), 1)
    light = (SPARE - extra + rank < LIGHT) & ~gone
    return jnp.max(jnp.sum(jnp.where(light, counts, 0).reshape(counts.shape[0], groups, OWN), 2))


def whole_kernel(first, place, mask, table, w_ref, x_ref, y_ref, d_ref, *rest):
    *outs, taken = rest
    r = place[0]
    row_blocks = w_ref.shape[0] // BLOCK
    side = lax.broadcasted_iota(jnp.int32, (BLOCK, TILE), 1) // BLOCK
    for i, ref in enumerate((x_ref, y_ref, d_ref)):

        @pl.when(table[2 * SLOTS + OWN] == i + 1)
        def _():
            taken[...] = ref[...]

    slot = first
    for out in outs:
        for t in range(out.shape[1] // TILE):
            halves = []
            for half in range(2):
                source, col = table[SLOTS + slot], table[slot]
                slot += 1
                own = jnp.minimum(source, OWN - 1)
                other = jnp.maximum(source - OWN, 0)
                halves.append((
                    source >= OWN, col, (source & 1) != half,
                    pl.ds(pl.multiple_of((own >> 1) * TILE, TILE), TILE),
                    pl.ds(pl.multiple_of((other >> 1) * TILE, TILE), TILE),
                ))

            def block(i, _):
                rows = pl.ds(pl.multiple_of(i * BLOCK, BLOCK), BLOCK)
                values = []
                for is_taken, col, swap, own, other in halves:
                    value = jnp.where(is_taken, taken[rows, other], w_ref[rows, own])
                    value = jnp.where(swap, swap_halves(value), value)
                    values.append(jnp.where(mask[r * row_blocks + i, col] != 0, value, jnp.zeros_like(value)))
                out[rows, t * TILE : (t + 1) * TILE] = jnp.where(side == 0, values[0], values[1])
                return 0

            lax.fori_loop(0, row_blocks, block, 0)


def whole_columns(first, widths, place, mask, table, weight, taken):
    rows, width = weight.shape[0], OWN * BLOCK
    full = lambda shape: pl.BlockSpec(shape, lambda i, place, mask, table: (0, 0))
    return pl.pallas_call(
        functools.partial(whole_kernel, first),
        grid_spec=pltpu.PrefetchScalarGridSpec(
            num_scalar_prefetch=3,
            grid=(1,),
            in_specs=[pl.BlockSpec((rows, width), lambda i, place, mask, table: (0, place[2]))]
            + [full(taken[0].shape)] * 3,
            out_specs=[full((rows, w * BLOCK)) for w in widths],
            scratch_shapes=[pltpu.VMEM(taken[0].shape, jnp.bfloat16)],
        ),
        out_shape=[jax.ShapeDtypeStruct((rows, w * BLOCK), jnp.bfloat16) for w in widths],
        cost_estimate=BRIEF,
        compiler_params=vmem(48),
    )(place, mask, table, weight, *taken)


def gelu(preact):
    return jax.nn.gelu(preact, approximate=True).astype(jnp.bfloat16)


def light_sources(me, mode):
    if mode == "near":
        return [(me, me >= 0), (me - 1, me >= 1), (me + 1, me <= 2)]
    side = jnp.where(me <= 1, 1, -1)
    middle = (me == 1) | (me == 2)
    return [(me + 2 * side, me >= 0), (me + 3 * side, ~middle)]


def light_kernel(mode, place, mask, table, *rest):
    nearest = mode == "near"
    n = 3 if nearest else 2
    pieces, rest = rest[: n if nearest else 2 * n], rest[n if nearest else 2 * n :]
    if nearest:
        here_ref, total, weight, blocks, lines, sems = rest
    else:
        here_ref, before, out_ref, total, weight, blocks, lines, sems, before_sem = rest
        load = pltpu.make_async_copy(before, total, before_sem)
    step = pl.program_id(0)
    row_blocks = weight.shape[0] // BLOCK
    zero = lines.shape[1] - BLOCK
    me = place[0]
    sources = light_sources(me, mode)

    def copies(i):
        slot = blocks.at[pl.ds(i * SIZE, SIZE)]
        if nearest:
            return [(sources[i][1], pltpu.make_async_copy(pieces[i], slot, sems.at[i]))]
        return [
            (sources[i][1] & (me <= 1 if k else me > 1), pltpu.make_async_copy(pieces[2 * i + k], slot, sems.at[i]))
            for k in range(2)
        ]

    @pl.when(step == 0)
    def _():
        for i in range(n):
            for there, copy in copies(i):
                pl.when(there)(copy.start)
        for half in range(2):
            lines[half, zero : zero + BLOCK, :] = jnp.zeros((BLOCK, TILE), jnp.bfloat16)
        if nearest:
            total[...] = jnp.zeros_like(total)
        else:
            load.start()

    for i in range(n):
        for there, copy in copies(i):
            pl.when((step == i) & there)(copy.wait)

    source, valid = sources[0]
    for i in range(1, n):
        source = jnp.where(step == i, sources[i][0], source)
        valid = jnp.where(step == i, sources[i][1], valid)

    @pl.when(valid)
    def _():
        side = lax.broadcasted_iota(jnp.int32, (BLOCK, TILE), 1) // BLOCK
        many = 10

        def spread(t, _):
            value = blocks[pl.ds(pl.multiple_of(step * SIZE + t * many * BLOCK, BLOCK), many * BLOCK), :]
            other = swap_halves(value)
            for k in range(many):
                first = pl.ds(pl.multiple_of(2 * (t * many + k) * BLOCK, BLOCK), BLOCK)
                second = pl.ds(pl.multiple_of(2 * (t * many + k) * BLOCK + BLOCK, BLOCK), BLOCK)
                rows = slice(k * BLOCK, (k + 1) * BLOCK)
                lines[0, first, :] = value[rows]
                lines[1, first, :] = other[rows]
                lines[0, second, :] = other[rows]
                lines[1, second, :] = value[rows]
            return 0

        lax.fori_loop(0, CAP // many, spread, 0)

        def pair(t, row):
            cols = [table[2 * t], table[2 * t + 1]]
            kept = [[mask[source * row_blocks + i, col] * BLOCK for i in range(row_blocks)] for col in cols]
            at = [row, row + sum(kept[0])]
            lanes = pl.ds(pl.multiple_of(t * TILE, TILE), TILE)
            for i in range(row_blocks):
                values = []
                for half in range(2):
                    rows = pl.multiple_of(jnp.where(kept[half][i] != 0, at[half], zero), BLOCK)
                    values.append(lines[half, pl.ds(rows, BLOCK), :])
                    at[half] = at[half] + kept[half][i]
                weight[i * BLOCK : (i + 1) * BLOCK, lanes] = jnp.where(side == 0, values[0], values[1])
            return at[1]

        lax.fori_loop(0, LIGHT // 2, pair, jnp.int32(0))
        if not nearest:
            pl.when(step == 0)(load.wait)
        for first in range(0, total.shape[0], ROW_TILE):
            rows = slice(first, first + ROW_TILE)
            total[rows, :] += jnp.dot(here_ref[rows, :], weight[...], preferred_element_type=jnp.float32)

    if not nearest:

        @pl.when(step == n - 1)
        def _():
            out_ref[...] = gelu(total[...])


def light_columns(mode, place, mask, table, pieces, here, before=None):
    rows, width = here.shape
    depth, columns = width // 4, LIGHT * BLOCK
    full = pl.BlockSpec((rows, columns), lambda i, *_: (0, 0))
    nearest = mode == "near"
    n = 3 if nearest else 2

    def block(i, place, *_):
        source = jnp.int32(0)
        last = jnp.int32(0)
        for k, (at, valid) in enumerate(light_sources(place[0], mode)):
            last = jnp.where(valid, at, last)
            source = jnp.where(i == k, last, source)
        return 0, source

    scratch = [
        pltpu.VMEM((depth, columns), jnp.bfloat16),
        pltpu.VMEM((n * SIZE, TILE), jnp.bfloat16),
        pltpu.VMEM((2, LIGHT * depth + BLOCK, TILE), jnp.bfloat16),
        pltpu.SemaphoreType.DMA((n,)),
    ]
    if not nearest:
        scratch = [pltpu.VMEM((rows, columns), jnp.float32), *scratch, pltpu.SemaphoreType.DMA]
    any_space = pl.BlockSpec(memory_space=pl.ANY)
    return pl.pallas_call(
        functools.partial(light_kernel, mode),
        grid_spec=pltpu.PrefetchScalarGridSpec(
            num_scalar_prefetch=3,
            grid=(n,),
            in_specs=[any_space] * len(pieces) + [pl.BlockSpec((rows, depth), block)] + ([] if nearest else [any_space]),
            out_specs=full,
            scratch_shapes=scratch,
        ),
        out_shape=jax.ShapeDtypeStruct((rows, columns), jnp.float32 if nearest else jnp.bfloat16),
        cost_estimate=BRIEF,
        compiler_params=vmem(52),
    )(place, mask, table, *pieces, here, *([] if nearest else [before]))


def early_kernel(place, *rest):
    *pieces, tokens_ref, total1, total2, weight, sems = rest
    columns = pieces[0].shape[1]
    step = pl.program_id(0)
    works = place[4] != 0
    copies = [
        pltpu.make_async_copy(piece, weight.at[i % 3, :, pl.ds((i // 3) * columns, columns)], sems.at[i])
        for i, piece in enumerate(pieces)
    ]

    @pl.when(works & (step == 0))
    def _():
        for copy in copies:
            copy.start()

    for k in range(3):

        @pl.when(works & (step == k))
        def _():
            copies[k].wait()
            if k < 2:
                copies[3 + k].wait()
            for first in range(0, total1.shape[0], ROW_TILE):
                rows = slice(first, first + ROW_TILE)
                here = tokens_ref.at[rows, :] if len(tokens_ref.shape) == 2 else tokens_ref.at[:, rows, :]
                value = tokens_dot(here, weight.at[k] if k < 2 else weight.at[k, :, :columns])
                if k == 0:
                    total1[rows, :] = value[:, :columns]
                    total2[rows, :] = value[:, columns:]
                else:
                    total1[rows, :] += value[:, :columns]
                    if k < 2:
                        total2[rows, :] += value[:, columns:]


def tokens_dot(tokens_ref, weight):
    if len(tokens_ref.shape) == 2:
        return jnp.dot(tokens_ref[...], weight[...], preferred_element_type=jnp.float32)
    parts, _, piece = tokens_ref.shape
    dots = [
        jnp.dot(tokens_ref[i], weight[i * piece : (i + 1) * piece, :], preferred_element_type=jnp.float32)
        for i in range(parts)
    ]
    return sum(dots[1:], dots[0])


def tokens_block(tokens, depth, rows, at):
    if tokens.ndim == 2:
        return pl.BlockSpec((rows, depth), lambda i, place: (at(i, place)[0], at(i, place)[1]))
    parts = depth // tokens.shape[2]
    return pl.BlockSpec((parts, rows, tokens.shape[2]), lambda i, place: (at(i, place)[1], at(i, place)[0], 0))


def early_products(place, pieces, tokens):
    depth, columns = pieces[0].shape
    rows = tokens.shape[-2]

    def at(i, place):
        return 0, jnp.where(i == 0, place[0], jnp.where(i == 1, place[1], place[2]))

    return pl.pallas_call(
        early_kernel,
        grid_spec=pltpu.PrefetchScalarGridSpec(
            num_scalar_prefetch=1,
            grid=(3,),
            in_specs=[pl.BlockSpec(memory_space=pl.ANY)] * 5 + [tokens_block(tokens, depth, rows, at)],
            out_specs=[pl.BlockSpec((rows, columns), lambda i, place: (0, 0))] * 2,
            scratch_shapes=[pltpu.VMEM((3, depth, 2 * columns), jnp.bfloat16), pltpu.SemaphoreType.DMA((5,))],
        ),
        out_shape=[jax.ShapeDtypeStruct((rows, columns), jnp.float32)] * 2,
        cost_estimate=BRIEF,
        compiler_params=vmem(48),
    )(place, *pieces, tokens)


def last_kernel(n, place, *rest):
    pieces, token_refs, rest = rest[:n], rest[n : 2 * n], rest[2 * n :]
    *totals, out_ref, weight, sems = rest
    works = place[4] != 0

    @pl.when(works & (pl.program_id(0) == 0))
    def _():
        copies = [pltpu.make_async_copy(piece, weight.at[i], sems.at[i]) for i, piece in enumerate(pieces)]
        for copy in copies:
            copy.start()
        for copy in copies:
            copy.wait()

    @pl.when(works)
    def _():
        terms = [total[...] for total in totals] + [tokens_dot(ref, weight.at[i]) for i, ref in enumerate(token_refs)]
        out_ref[...] = gelu(sum(terms[1:], terms[0]))


def last_products(place, pieces, tokens, *totals):
    n = len(pieces)
    depth, columns = pieces[0].shape
    rows = tokens.shape[-2]
    at = lambda k: lambda i, place: (i * place[4], place[k])
    return pl.pallas_call(
        functools.partial(last_kernel, n),
        grid_spec=pltpu.PrefetchScalarGridSpec(
            num_scalar_prefetch=1,
            grid=(rows // ROW_TILE,),
            in_specs=[pl.BlockSpec(memory_space=pl.ANY)] * n
            + [tokens_block(tokens, depth, ROW_TILE, at(k)) for k in range(4 - n, 4)]
            + [pl.BlockSpec((ROW_TILE, columns), lambda i, place: (i * place[4], 0))] * len(totals),
            out_specs=pl.BlockSpec((ROW_TILE, columns), lambda i, place: (i, 0)),
            scratch_shapes=[pltpu.VMEM((n, depth, columns), jnp.bfloat16), pltpu.SemaphoreType.DMA((n,))],
        ),
        out_shape=jax.ShapeDtypeStruct((rows, columns), jnp.bfloat16),
        cost_estimate=BRIEF,
        compiler_params=vmem(48),
    )(place, *pieces, *[tokens] * n, *totals)


def order_kernel(table, place, light, second_here, second_back, *rest):
    *sources, out_ref, results = rest
    at = light.shape[1] + second_here.shape[1]
    results[:, : light.shape[1]] = light[...]

    @pl.when(place[4] != 0)
    def _():
        results[:, light.shape[1] : at] = second_here[...]

    @pl.when(place[4] == 0)
    def _():
        results[:, light.shape[1] : at] = second_back[...]

    for ref in sources:
        results[:, at : at + ref.shape[1]] = ref[...]
        at += ref.shape[1]
    side = lax.broadcasted_iota(jnp.int32, (out_ref.shape[0], TILE), 1) // BLOCK
    for t in range(OWN // 2):
        values = []
        for half in range(2):
            slot = table[2 * SLOTS + 2 * t + half]
            value = results[:, pl.ds(pl.multiple_of((slot >> 1) * TILE, TILE), TILE)]
            values.append(jnp.where((slot & 1) == half, value, swap_halves(value)))
        out_ref[:, t * TILE : (t + 1) * TILE] = jnp.where(side == 0, values[0], values[1])


def in_order(table, place, sources):
    rows = sources[0].shape[0]
    tile = rows // 4
    widths = [s.shape[1] for s in sources]
    wide = sum(widths) - widths[1]
    return pl.pallas_call(
        order_kernel,
        grid_spec=pltpu.PrefetchScalarGridSpec(
            num_scalar_prefetch=2,
            grid=(4,),
            in_specs=[pl.BlockSpec((tile, w), lambda i, *_: (i, 0)) for w in widths],
            out_specs=pl.BlockSpec((tile, OWN * BLOCK), lambda i, *_: (i, 0)),
            scratch_shapes=[pltpu.VMEM((tile, wide), jnp.bfloat16)],
        ),
        out_shape=jax.ShapeDtypeStruct((rows, OWN * BLOCK), jnp.bfloat16),
        cost_estimate=BRIEF,
        compiler_params=vmem(32),
    )(table, place, *sources)


def line_body(tokens, up_weight, block_mask):
    depth, hidden_dev = up_weight.shape
    r, c, p = (lax.axis_index(a).astype(jnp.int32) for a in ("row", "col", "rep"))
    share = hidden_dev // CORES
    rows, width = tokens.shape
    parts = CHIPS * CORES
    piece = width // parts
    place = jnp.stack([r, c, p])
    is_middle = (r == 1) | (r == 2)

    given_mask = block_mask
    block_mask = jnp.pad(block_mask, ((0, 0), (0, 1)))
    counts = block_mask.reshape(lax.axis_size("row"), -1, block_mask.shape[1]).sum(1)
    count = counts.sum(0)
    table, shared, packed, own_heavy = pack_columns(place, block_mask, count, up_weight)
    most = most_packed(counts[:, :EMPTY], count[:EMPTY], shared)

    up1, down1 = lax.ppermute(packed, "row", UP), lax.ppermute(packed, "row", DOWN)
    handed = []
    for i in range(len(SWAPS)):
        other = c ^ (i + 1)
        k = other - (other > c).astype(jnp.int32)
        handed.append(lax.dynamic_slice_in_dim(up_weight, p * share + k * SPARE * BLOCK, SPARE * BLOCK, 1))
    taken = [lax.ppermute(handed[0], "col", SWAP_X), lax.ppermute(handed[1], "col", SWAP_Y)]
    mid2 = lax.ppermute(own_heavy, "row", MIDDLE)
    up1, down1, taken = lax.optimization_barrier((up1, down1, taken))
    up2, down2 = lax.ppermute(up1, "row", UP[1:]), lax.ppermute(down1, "row", DOWN[1:])
    taken.append(lax.ppermute(after(handed[2], taken), "col", SWAP_DIAGONAL))
    light = light_columns("near", place, block_mask, table, [packed, up1, down1], tokens)
    mine = lax.dynamic_slice_in_dim(tokens, (c * CORES + p) * piece, piece, 1)
    mine = lax.ppermute(after(mine, packed), "row", INWARD)
    end = lax.all_gather(after(mine, up2, down2, taken[2], light), ("col", "rep"), axis=0, tiled=True)
    (first,) = whole_columns(LIGHT + HEAVY, (HEAVY,), place, block_mask, table, up_weight, taken)
    near2 = lax.ppermute(after(own_heavy, mine, first), "row", INWARD)
    up2, down2, first, mine = lax.optimization_barrier((up2, down2, first, mine))
    up3, down3 = lax.ppermute(up2, "row", UP[2:]), lax.ppermute(down2, "row", DOWN[2:])
    mid1 = lax.ppermute(after(first, mid2), "row", MIDDLE)
    near1 = lax.ppermute(first, "row", INWARD)
    far1 = lax.ppermute(near1, "row", MIDDLE)
    at = jnp.stack([r, 3 - r, jnp.where(r <= 1, 0, 3), jnp.where(r <= 1, 3, 0), is_middle.astype(jnp.int32)])
    at = jnp.where(is_middle, at, jnp.zeros_like(at))
    early = [first, mid1, near1, own_heavy, mid2]
    here_total1, here_total2 = early_products(at, early, tokens)
    far2 = lax.ppermute(after(near2, near1, here_total1, up3, down3), "row", MIDDLE)
    pieces = [up2, down2, up3, down3]

    end = end.reshape(parts, rows, piece)
    first_end = last_products(at, [first, mid1, near1, far1], after(end, here_total1))
    back1 = lax.ppermute(first_end, "row", OUTWARD)
    first_here = last_products(at, [after(far1, first_end)], tokens, here_total1)
    second_end = last_products(at, [own_heavy, mid2, near2, after(far2, first_here)], end)
    back2 = lax.ppermute(second_end, "row", OUTWARD)
    hidden1 = jnp.where(is_middle, after(first_here, second_end), back1)
    second_here = last_products(at, [near2, after(far2, hidden1)], tokens, here_total2)
    home = [lax.ppermute(hidden1, "col", pairs) for pairs in SWAPS]
    light = light_columns("rest", place, block_mask, after(table, hidden1), pieces, tokens, light)
    results = [light, second_here, after(back2, *home), hidden1, *home]
    return lax.cond(
        most > 2 * CAP,
        lambda *_: gather_body(tokens, up_weight, given_mask),
        lambda table, *results: in_order(table, at, results),
        table, *results,
    )


def solution(mesh):
    in_specs = (P("row", None), P("row", "col"), P())
    out_specs = P("row", ("col", "rep"))

    def body(tokens, up_weight, block_mask):
        line = dict(mesh.shape) == {"row": 4, "col": CHIPS, "rep": CORES}
        line = line and up_weight.shape[1] == CORES * OWN * BLOCK and tokens.shape[0] % (4 * ROW_TILE) in (0, 2 * ROW_TILE)
        return (line_body if line else gather_body)(tokens, up_weight, block_mask)

    return jax.shard_map(body, mesh=mesh, in_specs=in_specs, out_specs=out_specs, check_vma=False)
```
